256 devices in a mesh: patch: 32 (over y, z_lo, core), guide: 8 (over x, z_hi).
Axes of the slice: x: 4, y: 4, z: 8 (z_hi: 2, z_lo: 4; z = z_hi * 4 + z_lo), core: 2. Of those that a mesh axis runs over, the one named last changes fastest.
Arguments:
- hidden_in: bfloat16 [8, 2048, 1152], P('guide', 'patch'), may hold values from -6 to 6
- stale_in: bfloat16 [8, 2048, 1152], P('guide', 'patch'), may hold values from -6 to 6
- modulation: float32 [8, 5, 1152], P('guide'), may hold values from -3 to 3
- latent: float32 [8, 256, 128], P('guide', 'patch'), may hold values from -6 to 6
- timestep: int32 [4], replicated, may hold values from 100 to 799
- w_qkv: bfloat16 [1152, 3456], replicated, may hold values from -1.26689965 to 1.26689965
- w_out: bfloat16 [1152, 1152], replicated, may hold values from -0.1875 to 0.1875
- w_final: bfloat16 [1152, 16], replicated, may hold values from -0.1875 to 0.1875
Outputs:
- next_latent: float32 [8, 256, 128], P('guide', 'patch')
The draws below stay inside these ranges and needn't reach their ends.
All inputs are finite; a program needn't handle non-finite values.
Results may differ from the reference program's by a relative error of at most 0.0025.
Values may be sent and summed in bfloat16 or wider, within the bound.
No kernel may reach another device: no remote copies, remote signals or barrier semaphores. Data moves between devices by JAX's collectives and lax.ppermute only.
A program may use at most 128 MiB of HBM per device.

```python
import math
import jax
import jax.numpy as jnp
from jax import lax

D = 1152
HEADS = 16
LAT = 16
STRIDE = 50
TOK_DEV = 64
TOKENS = 2048
GUIDES = 8
PAIRS = 4
N_PATCH = 32


def draw_w_qkv(key, part):
    key = jax.random.fold_in(key, 11)
    key_query, key_other, key_value = jax.random.split(key, 3)
    spread = D ** (-0.5)
    w_query = jnp.clip(jax.random.normal(key_query, (D, D), jnp.float32), -6.0, 6.0) * spread
    w_key = jnp.clip(jax.random.normal(key_other, (D, D), jnp.float32), -6.0, 6.0) * spread
    w_value = jnp.clip(jax.random.normal(key_value, (D, D), jnp.float32), -6.0, 6.0) * spread
    return jnp.concatenate([w_query, w_key, w_value], axis=1).astype(jnp.bfloat16)


def plant(result, own_key, smallest, top_value):
    place = [jax.random.randint(jax.random.fold_in(own_key, axis), (), 0, length) for axis, length in enumerate(result.shape)]
    main_axis = result.shape.index(max(result.shape))
    neighbour = place[:main_axis] + [(place[main_axis] + 1) % result.shape[main_axis]] + place[main_axis + 1:]
    return result.at[tuple(place)].set(smallest).at[tuple(neighbour)].set(top_value)


def levels(key, extent, cuts, least, largest):
    def one(axis_at, shards_of):
        steps = jax.random.uniform(jax.random.fold_in(jax.random.fold_in(key, 6), axis_at), (shards_of,), jnp.float32, least / len(cuts), largest / len(cuts))
        return jnp.repeat(jnp.exp(steps), extent[axis_at] // shards_of).reshape((-1,) + (1,) * (len(extent) - axis_at - 1))

    gain = one(*cuts[0])
    for cut in cuts[1:]:
        gain = gain * one(*cut)
    return gain


def scatter_about(rng, shape, scale, most, shards=(), kind=jnp.bfloat16):
    result = jax.random.normal(rng, shape, jnp.float32) * scale
    if len(shards) > 0:
        result = levels(rng, shape, shards, -0.22, 0.18) * result
    return jnp.clip(result, min=-most, max=most).astype(kind)


def setup_inputs(seed: int = 0) -> dict:
    arg_keys = jax.random.split(jax.random.key(seed), 9)
    hidden_in = scatter_about(arg_keys[0], (GUIDES, TOKENS, D), 1.0, 6.0, ((0, 8), (1, 32)))
    stale_in = scatter_about(arg_keys[1], (GUIDES, TOKENS, D), 1.0, 6.0, ((0, 8), (1, 32)))
    modulation = scatter_about(arg_keys[2], (GUIDES, 5, D), 0.5, 3.0, ((0, 8),), jnp.float32)
    latent = scatter_about(arg_keys[3], (GUIDES, TOKENS // 8, 128), 1.0, 6.0, ((0, 8), (1, 32)), jnp.float32)
    timestep = plant(jax.random.randint(arg_keys[4], (PAIRS,), 100, 800), jax.random.fold_in(arg_keys[4], 1), 100, 799).astype(jnp.int32)
    w_qkv = draw_w_qkv(jax.random.fold_in(arg_keys[8], 71), 0)
    w_out = scatter_about(arg_keys[6], (D, D), D ** -0.5, 0.1875)
    w_final = scatter_about(arg_keys[7], (D, LAT), D ** -0.5, 0.1875)
    return dict(hidden_in=hidden_in, stale_in=stale_in, modulation=modulation, latent=latent, timestep=timestep, w_qkv=w_qkv, w_out=w_out, w_final=w_final)


def layer_norm(values):
    mean = lax.optimization_barrier(jnp.mean(values, axis=-1, keepdims=True))
    centred = values - mean
    var = lax.optimization_barrier(jnp.mean(centred * centred, axis=-1, keepdims=True))
    return centred / jnp.sqrt(var + 1e-06)

def attend(queries, keys_values):
    width = queries.shape[1]
    head_size = width // HEADS
    query_heads = queries.reshape(-1, HEADS, head_size).astype(jnp.float32)
    key_heads = keys_values[:, :width].reshape(-1, HEADS, head_size).astype(jnp.float32)
    value_heads = keys_values[:, width:].reshape(-1, HEADS, head_size).astype(jnp.float32)
    scores = jnp.einsum('qhd,khd->hqk', query_heads, key_heads) * head_size ** (-0.5)
    top = lax.optimization_barrier(jnp.max(scores, axis=-1, keepdims=True))
    expo = jnp.exp(scores - top)
    prob = (expo / lax.optimization_barrier(jnp.sum(expo, axis=-1, keepdims=True))).astype(jnp.bfloat16)
    out = jnp.einsum('hqk,khd->qhd', prob.astype(jnp.float32), value_heads)
    return out.astype(jnp.bfloat16).reshape(-1, width)

def alpha_bar(step_index):
    angle = (step_index.astype(jnp.float32) / 1000.0 + 0.008) / 1.008 * (math.pi / 2.0)
    return jnp.cos(angle) ** 2

def reference(hidden_in, stale_in, modulation, latent, timestep, w_qkv, w_out, w_final):
    width = hidden_in.shape[2]
    noises = []
    for image in range(GUIDES):
        mod = modulation[image]
        source = hidden_in[image].astype(jnp.float32)
        attn_in = (layer_norm(source) * (1.0 + mod[1]) + mod[0]).astype(jnp.bfloat16)
        fresh = jnp.dot(attn_in, w_qkv, preferred_element_type=jnp.float32).astype(jnp.bfloat16)
        stale_kv = jnp.dot(stale_in[image], w_qkv[:, width:], preferred_element_type=jnp.float32).astype(jnp.bfloat16)

        def patch_attention(patch_id):
            start = (patch_id * TOK_DEV).astype(jnp.int32)
            queries = lax.dynamic_slice_in_dim(fresh[:, :width], start, TOK_DEV, 0)
            own = lax.dynamic_slice_in_dim(fresh[:, width:], start, TOK_DEV, 0)
            keys_values = lax.dynamic_update_slice_in_dim(stale_kv, own, start, 0)
            return attend(queries, keys_values)
        attended = lax.map(patch_attention, jnp.arange(N_PATCH, dtype=jnp.int32)).reshape(-1, width)
        mixed = source + mod[2] * jnp.dot(attended, w_out, preferred_element_type=jnp.float32)
        final_in = (layer_norm(mixed) * (1.0 + mod[4]) + mod[3]).astype(jnp.bfloat16)
        noise = jnp.dot(final_in, w_final, preferred_element_type=jnp.float32)
        noises.append(noise.reshape(-1, 128))
    results = []
    for image in range(GUIDES):
        pair = image // 2
        cond = noises[2 * pair]
        uncond = noises[2 * pair + 1]
        guided = uncond + 4.5 * (cond - uncond)
        now = timestep[pair]
        bar_now = alpha_bar(now)
        bar_prev = alpha_bar(now - STRIDE)
        clean = (latent[image] - jnp.sqrt(1.0 - bar_now) * guided) / jnp.sqrt(bar_now)
        results.append(jnp.sqrt(bar_prev) * clean + jnp.sqrt(1.0 - bar_prev) * guided)
    return jnp.stack(results, axis=0)
```

```python
import functools
import math

import jax
import jax.numpy as jnp
from jax import lax
from jax.experimental import pallas as pl
from jax.experimental.pallas import tpu as pltpu
from jax.sharding import PartitionSpec as P

HEADS = 16
HEAD = 72
WIDTH = 1152
STRIDE = 50
NY, NZ, NC = 4, 4, 2
STATS = 128
BF16, F32 = jnp.bfloat16, jnp.float32
VMEM_LIMIT = 48 * 1024 * 1024


def layer_norm(values):
    mean = jnp.mean(values, axis=-1, keepdims=True)
    centred = values - mean
    var = jnp.mean(centred * centred, axis=-1, keepdims=True)
    return centred / jnp.sqrt(var + 1e-06)


def alpha_bar(step_index):
    angle = (step_index.astype(F32) / 1000.0 + 0.008) / 1.008 * (math.pi / 2.0)
    return jnp.cos(angle) ** 2


def patch_pairs(dy, dz, dc):
    pairs = []
    for y in range(NY):
        for z in range(NZ):
            for c in range(NC):
                target = (((y + dy) % NY) * NZ + (z + dz) % NZ) * NC + (c + dc) % NC
                pairs.append(((y * NZ + z) * NC + c, target))
    return pairs


def send(value, dy=0, dz=0, dc=0):
    return lax.ppermute(value, "patch", patch_pairs(dy, dz, dc))


def fresh_kernel(hidden_ref, mod_ref, w_ref, out_ref, attn_in):
    @pl.when(pl.program_id(0) == 0)
    def _():
        source = hidden_ref[...].astype(F32)
        attn_in[...] = (
            layer_norm(source) * (1.0 + mod_ref[1:2, :]) + mod_ref[0:1, :]
        ).astype(BF16)

    out_ref[...] = jnp.dot(
        attn_in[...], w_ref[...], preferred_element_type=F32
    ).astype(BF16)


def project_fresh(hidden, mod, w_qkv):
    rows, width = hidden.shape
    cols = w_qkv.shape[1]
    block = 384
    return pl.pallas_call(
        fresh_kernel,
        grid=(cols // block,),
        in_specs=[
            pl.BlockSpec((rows, width), lambda i: (0, 0)),
            pl.BlockSpec(mod.shape, lambda i: (0, 0)),
            pl.BlockSpec((width, block), lambda i: (0, i)),
        ],
        out_specs=pl.BlockSpec((rows, block), lambda i: (0, i)),
        out_shape=jax.ShapeDtypeStruct((rows, cols), BF16),
        scratch_shapes=[pltpu.VMEM((rows, width), BF16)],
        compiler_params=pltpu.CompilerParams(vmem_limit_bytes=VMEM_LIMIT),
        cost_estimate=pl.CostEstimate(
            flops=2 * rows * width * cols, bytes_accessed=2 * width * cols, transcendentals=0
        ),
        name="fresh_qkv",
    )(hidden, mod, w_qkv)


def head_window(head):
    start = min(head * HEAD // 128 * 128, WIDTH - 256)
    return start, head * HEAD - start


def attend_kernel(own, *refs):
    if own:
        q_ref, kv_ref, fresh_ref, out_ref, acc = refs
    else:
        q_ref, kv_ref, out_ref, acc = refs
    rows = q_ref.shape[0]
    scale = HEAD ** (-0.5)
    lane = lax.broadcasted_iota(jnp.int32, (rows, 256), 1)
    stat_lane = lax.broadcasted_iota(jnp.int32, (rows, STATS), 1)
    stats = jnp.zeros((rows, STATS), F32)
    acc[...] = jnp.zeros_like(acc)

    def keyval(start):
        cols = pl.ds(start, 256)
        if own:
            n_own = fresh_ref.shape[0]
            return jnp.concatenate([fresh_ref[:, cols], kv_ref[n_own:, cols]], axis=0)
        return kv_ref[:, cols]

    for head in range(HEADS):
        start, offset = head_window(head)
        inside = (lane >= offset) & (lane < offset + HEAD)
        query = jnp.where(inside, q_ref[:, start : start + 256], jnp.zeros((), BF16))
        scores = lax.dot_general(
            query, keyval(start), (((1,), (1,)), ((), ())), preferred_element_type=F32
        ) * scale
        top = jnp.max(scores, axis=-1, keepdims=True)
        expo = jnp.exp(scores - top)
        total = jnp.sum(expo, axis=-1, keepdims=True)
        value = jnp.dot(expo.astype(BF16), keyval(WIDTH + start), preferred_element_type=F32)
        value = jnp.where(inside, value / total, 0.0)
        acc[:, start : start + 256] += value
        stats = jnp.where(stat_lane % HEADS == head, top + jnp.log(total), stats)
    high = stats.astype(BF16)
    rest = stats - high.astype(F32)
    middle = rest.astype(BF16)
    low = (rest - middle.astype(F32)).astype(BF16)
    packed = jnp.where(
        stat_lane < HEADS,
        high.astype(F32),
        jnp.where(
            stat_lane < 2 * HEADS,
            middle.astype(F32),
            jnp.where(stat_lane < 3 * HEADS, low.astype(F32), 0.0),
        ),
    )
    out_ref[:, :WIDTH] = acc[...].astype(BF16)
    out_ref[:, WIDTH:] = packed.astype(BF16)


def attend(query, keyval, fresh=None):
    rows = query.shape[0]
    keys = keyval.shape[0]
    args = (query, keyval) if fresh is None else (query, keyval, fresh)
    return pl.pallas_call(
        functools.partial(attend_kernel, fresh is not None),
        in_specs=[pl.BlockSpec(memory_space=pltpu.VMEM)] * len(args),
        out_specs=pl.BlockSpec(memory_space=pltpu.VMEM),
        out_shape=jax.ShapeDtypeStruct((rows, WIDTH + STATS), BF16),
        scratch_shapes=[pltpu.VMEM((rows, WIDTH), F32)],
        compiler_params=pltpu.CompilerParams(vmem_limit_bytes=VMEM_LIMIT),
        cost_estimate=pl.CostEstimate(
            flops=4 * HEADS * rows * keys * 256,
            bytes_accessed=4 * keys * WIDTH,
            transcendentals=HEADS * rows * keys,
        ),
        name="attend_own" if fresh is not None else "attend",
    )(*args)


def post_kernel(p0, p1, p2, p3, hidden_ref, mod_ref, w_out_ref, w_final_ref, out_ref):
    row = lax.broadcasted_iota(jnp.int32, (STATS, WIDTH), 0)
    col = lax.broadcasted_iota(jnp.int32, (STATS, WIDTH), 1)
    offset = col - (row % HEADS) * HEAD
    pick = (row < 3 * HEADS) & (offset >= 0) & (offset < HEAD)
    pick = jnp.where(pick, 1.0, 0.0).astype(BF16)
    parts = (p0, p1, p2, p3)
    sums = [jnp.dot(p[:, WIDTH:], pick, preferred_element_type=F32) for p in parts]
    top = functools.reduce(jnp.maximum, sums)
    weights = [jnp.exp(s - top) for s in sums]
    total = functools.reduce(jnp.add, weights)
    mix = functools.reduce(
        jnp.add, [w * p[:, :WIDTH].astype(F32) for w, p in zip(weights, parts)]
    )
    attended = (mix / total).astype(BF16)
    source = hidden_ref[...].astype(F32)
    mixed = source + mod_ref[2:3, :] * jnp.dot(
        attended, w_out_ref[...], preferred_element_type=F32
    )
    final_in = (layer_norm(mixed) * (1.0 + mod_ref[4:5, :]) + mod_ref[3:4, :]).astype(BF16)
    wide = jnp.dot(final_in, w_final_ref[...], preferred_element_type=F32)
    rows = wide.shape[0]
    token = lax.broadcasted_iota(jnp.int32, wide.shape, 0) % 8
    place = lax.broadcasted_iota(jnp.int32, wide.shape, 1) // 16
    wide = jnp.where(token == place, wide, 0.0)
    out_ref[...] = jnp.sum(wide.reshape(rows // 8, 8, 128), axis=1)


def post(parts, hidden, mod, w_out, w_final_wide):
    rows = hidden.shape[0]
    return pl.pallas_call(
        post_kernel,
        in_specs=[pl.BlockSpec(memory_space=pltpu.VMEM)] * 8,
        out_specs=pl.BlockSpec(memory_space=pltpu.VMEM),
        out_shape=jax.ShapeDtypeStruct((rows // 8, 128), F32),
        compiler_params=pltpu.CompilerParams(vmem_limit_bytes=VMEM_LIMIT),
        cost_estimate=pl.CostEstimate(
            flops=2 * rows * WIDTH * WIDTH, bytes_accessed=2 * WIDTH * WIDTH, transcendentals=0
        ),
        name="post",
    )(*parts, hidden, mod, w_out, w_final_wide)


def body(hidden_in, stale_in, modulation, latent, timestep, w_qkv, w_out, w_final):
    image = lax.axis_index("guide")
    hidden, stale, mod = hidden_in[0], stale_in[0], modulation[0]

    stale_z = [send(stale, dz=k) for k in (2, 1, 3)]
    w_final_wide = jnp.tile(w_final, (1, 8))
    now = timestep[image // 2]
    bar_now = alpha_bar(now)
    bar_prev = alpha_bar(now - STRIDE)
    latent_gain = jnp.sqrt(bar_prev) / jnp.sqrt(bar_now)
    noise_gain = jnp.sqrt(1.0 - bar_prev) - latent_gain * jnp.sqrt(1.0 - bar_now)

    fresh = project_fresh(hidden, mod, w_qkv)
    query = fresh[:, :WIDTH]
    fresh_kv = fresh[:, WIDTH:]
    query_y = [send(query, dy=k) for k in (2, 1, 3)]

    mine = jnp.concatenate([stale] + stale_z, axis=0)
    other = send(mine, dc=1)
    keys_in = jnp.concatenate([mine, other], axis=0)
    keyval = jnp.dot(keys_in, w_qkv[:, WIDTH:], preferred_element_type=F32).astype(BF16)

    back = []
    for q, k in zip(query_y, (2, 1, 3)):
        back.append(send(attend(q, keyval), dy=-k))
    own = attend(query, keyval, fresh_kv)
    noise = post([own] + back, hidden, mod, w_out, w_final_wide)

    partner = lax.ppermute(
        noise, "guide", [(i, i ^ 1) for i in range(lax.axis_size("guide"))]
    )
    is_cond = image % 2 == 0
    cond = jnp.where(is_cond, noise, partner)
    uncond = jnp.where(is_cond, partner, noise)
    guided = uncond + 4.5 * (cond - uncond)
    return (latent_gain * latent[0] + noise_gain * guided)[None]


def solution(mesh):
    in_specs = (
        P("guide", "patch", None),
        P("guide", "patch", None),
        P("guide", None, None),
        P("guide", "patch", None),
        P(),
        P(),
        P(),
        P(),
    )
    out_specs = P("guide", "patch", None)
    return jax.shard_map(body, mesh=mesh, in_specs=in_specs, out_specs=out_specs, check_vma=False)
```

```python
import functools
import math

import jax
import jax.numpy as jnp
from jax import lax
from jax.experimental import pallas as pl
from jax.experimental.pallas import tpu as pltpu
from jax.sharding import PartitionSpec as P

HEADS = 16
HEAD = 72
WIDTH = 1152
STRIDE = 50
NY, NZ, NC = 4, 4, 2
STATS = 128
CHUNK = 384
BF16, F32 = jnp.bfloat16, jnp.float32
VMEM_LIMIT = 32 * 1024 * 1024


def layer_norm(values):
    mean = jnp.mean(values, axis=-1, keepdims=True)
    centred = values - mean
    var = jnp.mean(centred * centred, axis=-1, keepdims=True)
    return centred / jnp.sqrt(var + 1e-06)


def alpha_bar(step_index):
    angle = (step_index.astype(F32) / 1000.0 + 0.008) / 1.008 * (math.pi / 2.0)
    return jnp.cos(angle) ** 2


def patch_pairs(dy, dz, dc):
    pairs = []
    for y in range(NY):
        for z in range(NZ):
            for c in range(NC):
                target = (((y + dy) % NY) * NZ + (z + dz) % NZ) * NC + (c + dc) % NC
                pairs.append(((y * NZ + z) * NC + c, target))
    return pairs


def send(value, dy=0, dz=0, dc=0):
    return lax.ppermute(value, "patch", patch_pairs(dy, dz, dc))


def selector_kernel(out_ref):
    row = lax.broadcasted_iota(jnp.int32, (STATS, WIDTH), 0)
    col = lax.broadcasted_iota(jnp.int32, (STATS, WIDTH), 1)
    offset = col - (row % HEADS) * HEAD
    pick = (row < 3 * HEADS) & (offset >= 0) & (offset < HEAD)
    out_ref[...] = jnp.where(pick, 1.0, 0.0).astype(BF16)


def head_selector():
    return pl.pallas_call(
        selector_kernel,
        out_specs=pl.BlockSpec(memory_space=pltpu.VMEM),
        out_shape=jax.ShapeDtypeStruct((STATS, WIDTH), BF16),
        compiler_params=pltpu.CompilerParams(vmem_limit_bytes=4 * 1024 * 1024),
        cost_estimate=pl.CostEstimate(
            flops=2 * 10**10, bytes_accessed=4 * 10**7, transcendentals=0
        ),
        name="head_selector",
    )()


def fresh_kernel(hidden_ref, mod_ref, w_ref, out_ref):
    source = hidden_ref[...].astype(F32)
    attn_in = (layer_norm(source) * (1.0 + mod_ref[1]) + mod_ref[0]).astype(BF16)
    for start in range(0, w_ref.shape[1], CHUNK):
        out_ref[:, start : start + CHUNK] = jnp.dot(
            attn_in, w_ref[:, start : start + CHUNK], preferred_element_type=F32
        ).astype(BF16)


def project_fresh(hidden, mod, w_qkv):
    rows, width = hidden.shape
    cols = w_qkv.shape[1]
    return pl.pallas_call(
        fresh_kernel,
        in_specs=[pl.BlockSpec(memory_space=pltpu.VMEM)] * 3,
        out_specs=pl.BlockSpec(memory_space=pltpu.VMEM),
        out_shape=jax.ShapeDtypeStruct((rows, cols), BF16),
        compiler_params=pltpu.CompilerParams(vmem_limit_bytes=VMEM_LIMIT),
        cost_estimate=pl.CostEstimate(
            flops=2 * rows * width * cols, bytes_accessed=2 * width * cols, transcendentals=0
        ),
        name="fresh_qkv",
    )(hidden, mod, w_qkv)


def stale_kernel(first, x0, x1, x2, x3, w_ref, out_ref):
    keys = jnp.concatenate([x0[...], x1[...], x2[...], x3[...]], axis=0)
    for start in range(0, out_ref.shape[1], CHUNK):
        out_ref[:, start : start + CHUNK] = jnp.dot(
            keys,
            w_ref[:, first + start : first + start + CHUNK],
            preferred_element_type=F32,
        ).astype(BF16)


def project_stale(blocks, w_qkv, first, name):
    rows = len(blocks) * blocks[0].shape[0]
    width = w_qkv.shape[0]
    return pl.pallas_call(
        functools.partial(stale_kernel, first),
        in_specs=[pl.BlockSpec(memory_space=pltpu.VMEM)] * 5,
        out_specs=pl.BlockSpec(memory_space=pltpu.VMEM),
        out_shape=jax.ShapeDtypeStruct((rows, width), BF16),
        compiler_params=pltpu.CompilerParams(vmem_limit_bytes=VMEM_LIMIT),
        cost_estimate=pl.CostEstimate(
            flops=2 * rows * width * width, bytes_accessed=2 * width * width, transcendentals=0
        ),
        name=name,
    )(*blocks, w_qkv)


WINDOWS = (
    (0, (0, 1, 2)),
    (128, (3, 4)),
    (256, (5, 6)),
    (384, (7,)),
    (512, (8,)),
    (640, (9, 10, 11)),
    (768, (12,)),
    (896, (13, 14, 15)),
)


def attend_kernel(q_ref, k_mine, k_other, v_mine, v_other, out_ref, fresh_ref=None):
    rows = q_ref.shape[0]
    scale = HEAD ** (-0.5)
    lane = lax.broadcasted_iota(jnp.int32, (rows, 256), 1)
    stat_lane = lax.broadcasted_iota(jnp.int32, (rows, STATS), 1)
    stats = jnp.zeros((rows, STATS), F32)
    blocks = [None] * (WIDTH // 128)

    def window(mine_ref, other_ref, first, start):
        cols = slice(start, start + 256)
        if fresh_ref is not None:
            n_own = fresh_ref.shape[0]
            pieces = [fresh_ref[:, first + start : first + start + 256], mine_ref[n_own:, cols]]
        else:
            pieces = [mine_ref[:, cols]]
        return jnp.concatenate(pieces + [other_ref[:, cols]], axis=0)

    def inside(start, head):
        first = head * HEAD - start
        return (lane >= first) & (lane < first + HEAD)

    for part in (WINDOWS[:4], WINDOWS[4:]):
        scores = []
        for start, heads in part:
            query = q_ref[:, start : start + 256]
            zero = jnp.zeros((), BF16)
            stack = [jnp.where(inside(start, head), query, zero) for head in heads]
            scores.append(
                lax.dot_general(
                    jnp.concatenate(stack, axis=0),
                    window(k_mine, k_other, WIDTH, start),
                    (((1,), (1,)), ((), ())),
                    preferred_element_type=F32,
                )
            )
        tops = [jnp.max(s, axis=-1, keepdims=True) for s in scores]
        expos = [jnp.exp((s - t) * scale) for s, t in zip(scores, tops)]
        totals = [jnp.sum(e, axis=-1, keepdims=True) for e in expos]
        for (start, heads), top, expo, total in zip(part, tops, expos, totals):
            value = jnp.dot(
                expo.astype(BF16),
                window(v_mine, v_other, 2 * WIDTH, start),
                preferred_element_type=F32,
            )
            value = value * (1.0 / total)
            stat = top * scale + jnp.log(total)
            for n, head in enumerate(heads):
                mine = slice(n * rows, (n + 1) * rows)
                picked = jnp.where(inside(start, head), value[mine], 0.0)
                for j in (0, 1):
                    block = start // 128 + j
                    piece = picked[:, 128 * j : 128 * j + 128]
                    blocks[block] = piece if blocks[block] is None else blocks[block] + piece
                stats = jnp.where(stat_lane % HEADS == head, stat[mine], stats)
    high = stats.astype(BF16)
    rest = stats - high.astype(F32)
    middle = rest.astype(BF16)
    low = (rest - middle.astype(F32)).astype(BF16)
    split = stat_lane // HEADS
    packed = jnp.where(split == 2, low.astype(F32), 0.0)
    packed = jnp.where(split == 1, middle.astype(F32), packed)
    packed = jnp.where(split == 0, high.astype(F32), packed)
    for block, values in enumerate(blocks):
        out_ref[:, 128 * block : 128 * block + 128] = values.astype(BF16)
    out_ref[:, WIDTH:] = packed.astype(BF16)


def attend_cost(rows, keys):
    return pl.CostEstimate(
        flops=4 * HEADS * rows * keys * 256,
        bytes_accessed=4 * keys * WIDTH,
        transcendentals=HEADS * rows * keys,
    )


def attend(query, keyval):
    rows = query.shape[0]
    return pl.pallas_call(
        attend_kernel,
        in_specs=[pl.BlockSpec(memory_space=pltpu.VMEM)] * 5,
        out_specs=pl.BlockSpec(memory_space=pltpu.VMEM),
        out_shape=jax.ShapeDtypeStruct((rows, WIDTH + STATS), BF16),
        compiler_params=pltpu.CompilerParams(vmem_limit_bytes=VMEM_LIMIT),
        cost_estimate=attend_cost(rows, 2 * keyval[0].shape[0]),
        name="attend",
    )(query, *keyval)


def attend_own_kernel(
    q_ref, k_mine, k_other, v_mine, v_other, fresh_ref, time_ref, latent_ref,
    out_ref, base_ref, gain_ref,
):
    image = lax.axis_index("guide")
    now = jnp.full(latent_ref.shape, time_ref[image // 2], jnp.int32)
    bar_now = alpha_bar(now)
    bar_prev = alpha_bar(now - STRIDE)
    latent_gain = jnp.sqrt(bar_prev) / jnp.sqrt(bar_now)
    noise_gain = jnp.sqrt(1.0 - bar_prev) - latent_gain * jnp.sqrt(1.0 - bar_now)
    is_cond = jnp.full(latent_ref.shape, image % 2, jnp.int32) == 0
    base_ref[...] = latent_gain * latent_ref[...]
    gain_ref[0] = noise_gain * jnp.where(is_cond, 4.5, -3.5)
    gain_ref[1] = noise_gain * jnp.where(is_cond, -3.5, 4.5)
    attend_kernel(q_ref, k_mine, k_other, v_mine, v_other, out_ref, fresh_ref)


def attend_own(query, keyval, fresh, timestep, latent):
    rows = query.shape[0]
    vmem = pl.BlockSpec(memory_space=pltpu.VMEM)
    return pl.pallas_call(
        attend_own_kernel,
        in_specs=[vmem] * 6 + [pl.BlockSpec(memory_space=pltpu.SMEM), vmem],
        out_specs=[vmem] * 3,
        out_shape=[
            jax.ShapeDtypeStruct((rows, WIDTH + STATS), BF16),
            jax.ShapeDtypeStruct(latent.shape, F32),
            jax.ShapeDtypeStruct((2, *latent.shape), F32),
        ],
        compiler_params=pltpu.CompilerParams(vmem_limit_bytes=VMEM_LIMIT),
        cost_estimate=attend_cost(rows, 2 * keyval[0].shape[0]),
        name="attend_own",
    )(query, *keyval, fresh, timestep, latent)


def post_kernel(
    p0, p1, p2, p3, hidden_ref, mod_ref, w_out_ref, w_final_ref, scaled_ref, gain_ref,
    pick_ref, noise_ref, base_ref,
):
    pick = pick_ref[...]
    parts = (p0, p1, p2, p3)
    sums = [jnp.dot(p[:, WIDTH:], pick, preferred_element_type=F32) for p in parts]
    top = functools.reduce(jnp.maximum, sums)
    weights = [jnp.exp(s - top) for s in sums]
    total = functools.reduce(jnp.add, weights)
    mix = functools.reduce(
        jnp.add, [w * p[:, :WIDTH].astype(F32) for w, p in zip(weights, parts)]
    )
    attended = (mix / total).astype(BF16)
    source = hidden_ref[...].astype(F32)
    mixed = source + mod_ref[2] * jnp.dot(
        attended, w_out_ref[...], preferred_element_type=F32
    )
    final_in = (layer_norm(mixed) * (1.0 + mod_ref[4]) + mod_ref[3]).astype(BF16)
    w_wide = jnp.concatenate([w_final_ref[...]] * 8, axis=0)
    wide = lax.dot_general(
        final_in, w_wide, (((1,), (1,)), ((), ())), preferred_element_type=F32
    )
    rows = wide.shape[0]
    token = lax.broadcasted_iota(jnp.int32, wide.shape, 0) % 8
    place = lax.broadcasted_iota(jnp.int32, wide.shape, 1) // 16
    wide = jnp.where(token == place, wide, 0.0)
    noise = jnp.sum(wide.reshape(rows // 8, 8, 128), axis=1)
    noise_ref[...] = noise
    base_ref[...] = scaled_ref[...] + gain_ref[0] * noise


def post(parts, hidden, mod, w_out, w_final_t, scaled, gain, pick):
    rows = parts[0].shape[0]
    return pl.pallas_call(
        post_kernel,
        in_specs=[pl.BlockSpec(memory_space=pltpu.VMEM)] * 11,
        out_specs=[pl.BlockSpec(memory_space=pltpu.VMEM)] * 2,
        out_shape=[jax.ShapeDtypeStruct(scaled.shape, F32)] * 2,
        compiler_params=pltpu.CompilerParams(vmem_limit_bytes=VMEM_LIMIT),
        cost_estimate=pl.CostEstimate(
            flops=2 * rows * WIDTH * WIDTH, bytes_accessed=2 * WIDTH * WIDTH, transcendentals=0
        ),
        name="post",
    )(*parts, hidden, mod, w_out, w_final_t, scaled, gain, pick)


def body(hidden_in, stale_in, modulation, latent, timestep, w_qkv, w_out, w_final):
    hidden, stale = hidden_in[0], stale_in[0]
    mod = jnp.transpose(modulation, (1, 0, 2))
    rows = hidden.shape[0]

    stale, pick = lax.optimization_barrier((stale, head_selector()))
    stale_z = [send(stale, dz=k) for k in (2, 1, 3)]
    fresh = project_fresh(hidden, mod, w_qkv)
    query = fresh[:, :WIDTH]
    query_y = [send(query, dy=k) for k in (2, 1, 3)]

    blocks = [stale] + stale_z
    blocks, query_y[0] = lax.optimization_barrier((blocks, query_y[0]))
    k_mine = project_stale(blocks, w_qkv, WIDTH, "stale_keys")
    k_other = send(k_mine, dc=1)
    blocks, k_mine, query_y = lax.optimization_barrier((blocks, k_mine, query_y))
    v_mine = project_stale(blocks, w_qkv, 2 * WIDTH, "stale_values")
    v_other = send(v_mine, dc=1)
    keyval = (k_mine, k_other, v_mine, v_other)

    partial = attend(jnp.concatenate(query_y, axis=0), keyval)
    back = [
        send(partial[n * rows : (n + 1) * rows], dy=-k) for n, k in enumerate((2, 1, 3))
    ]
    own, scaled, gain = attend_own(query, keyval, fresh, timestep, latent[0])
    noise, base = post([own] + back, hidden, mod, w_out, w_final.T, scaled, gain, pick)
    partner = lax.ppermute(
        noise, "guide", [(i, i ^ 1) for i in range(lax.axis_size("guide"))]
    )
    return (base + gain[1] * partner)[None]


def solution(mesh):
    in_specs = (
        P("guide", "patch", None),
        P("guide", "patch", None),
        P("guide", None, None),
        P("guide", "patch", None),
        P(),
        P(),
        P(),
        P(),
    )
    out_specs = P("guide", "patch", None)
    return jax.shard_map(body, mesh=mesh, in_specs=in_specs, out_specs=out_specs, check_vma=False)
```

```python
import functools
import math

import jax
import jax.numpy as jnp
from jax import lax
from jax.experimental import pallas as pl
from jax.experimental.pallas import tpu as pltpu
from jax.sharding import PartitionSpec as P

HEADS = 16
HEAD = 72
WIDTH = 1152
STRIDE = 50
NY, NZ, NC = 4, 4, 2
STATS = 128
CHUNK = 384
BF16, F32 = jnp.bfloat16, jnp.float32
VMEM_LIMIT = 32 * 1024 * 1024


def layer_norm(values):
    mean = jnp.mean(values, axis=-1, keepdims=True)
    centred = values - mean
    var = jnp.mean(centred * centred, axis=-1, keepdims=True)
    return centred / jnp.sqrt(var + 1e-06)


def alpha_bar(step_index):
    angle = (step_index.astype(F32) / 1000.0 + 0.008) / 1.008 * (math.pi / 2.0)
    return jnp.cos(angle) ** 2


def send(value, route):
    pairs = []
    for y in range(NY):
        for z in range(NZ):
            for c in range(NC):
                ty, tz, tc = route(y, z, c)
                pairs.append(((y * NZ + z) * NC + c, ((ty % NY) * NZ + tz) * NC + tc))
    return lax.ppermute(value, "patch", pairs)


def z_xor(mask):
    return lambda y, z, c: (y, z ^ mask, c)


def other_core(y, z, c):
    return y, z, c ^ 1


def y_shift(step):
    return lambda y, z, c: (y + step, z, c)


def selector_kernel(out_ref):
    row = lax.broadcasted_iota(jnp.int32, (STATS, WIDTH), 0)
    col = lax.broadcasted_iota(jnp.int32, (STATS, WIDTH), 1)
    offset = col - (row % HEADS) * HEAD
    pick = (row < 3 * HEADS) & (offset >= 0) & (offset < HEAD)
    out_ref[...] = jnp.where(pick, 1.0, 0.0).astype(BF16)


def head_selector():
    return pl.pallas_call(
        selector_kernel,
        out_specs=pl.BlockSpec(memory_space=pltpu.VMEM),
        out_shape=jax.ShapeDtypeStruct((STATS, WIDTH), BF16),
        compiler_params=pltpu.CompilerParams(vmem_limit_bytes=4 * 1024 * 1024),
        cost_estimate=pl.CostEstimate(
            flops=2 * 10**10, bytes_accessed=4 * 10**7, transcendentals=0
        ),
        name="head_selector",
    )()


def fresh_kernel(hidden_ref, mod_ref, w_ref, out_ref):
    source = hidden_ref[...].astype(F32)
    attn_in = (layer_norm(source) * (1.0 + mod_ref[1]) + mod_ref[0]).astype(BF16)
    for start in range(0, w_ref.shape[1], CHUNK):
        out_ref[:, start : start + CHUNK] = jnp.dot(
            attn_in, w_ref[:, start : start + CHUNK], preferred_element_type=F32
        ).astype(BF16)


def project_fresh(hidden, mod, w_qkv):
    rows, width = hidden.shape
    cols = w_qkv.shape[1]
    return pl.pallas_call(
        fresh_kernel,
        in_specs=[pl.BlockSpec(memory_space=pltpu.VMEM)] * 3,
        out_specs=pl.BlockSpec(memory_space=pltpu.VMEM),
        out_shape=jax.ShapeDtypeStruct((rows, cols), BF16),
        compiler_params=pltpu.CompilerParams(vmem_limit_bytes=VMEM_LIMIT),
        cost_estimate=pl.CostEstimate(
            flops=2 * rows * width * cols, bytes_accessed=2 * width * cols, transcendentals=0
        ),
        name="fresh_qkv",
    )(hidden, mod, w_qkv)


def stale_kernel(*refs):
    *blocks, w_ref, out_ref = refs
    keys = jnp.concatenate([x[...] for x in blocks], axis=0)
    for start in range(0, out_ref.shape[1], CHUNK):
        out_ref[:, start : start + CHUNK] = jnp.dot(
            keys,
            w_ref[:, WIDTH + start : WIDTH + start + CHUNK],
            preferred_element_type=F32,
        ).astype(BF16)


def project_stale(blocks, w_qkv, flops):
    rows = len(blocks) * blocks[0].shape[0]
    width, cols = w_qkv.shape
    cols -= width
    return pl.pallas_call(
        stale_kernel,
        in_specs=[pl.BlockSpec(memory_space=pltpu.VMEM)] * (len(blocks) + 1),
        out_specs=pl.BlockSpec(memory_space=pltpu.VMEM),
        out_shape=jax.ShapeDtypeStruct((rows, cols), BF16),
        compiler_params=pltpu.CompilerParams(vmem_limit_bytes=VMEM_LIMIT),
        cost_estimate=pl.CostEstimate(
            flops=flops, bytes_accessed=1, transcendentals=0
        ),
        name="stale_kv",
    )(*blocks, w_qkv)


def gather_kernel(counts, *refs):
    first = 0
    for out_ref, count in zip(refs[sum(counts) :], counts):
        for n in range(count):
            block = refs[first + n]
            rows = block.shape[0]
            out_ref[n * rows : (n + 1) * rows, :] = block[...]
        first += count


def gather_blocks(*groups):
    blocks = [block for group in groups for block in group]
    rows, width = blocks[0].shape
    counts = tuple(len(group) for group in groups)
    vmem = pl.BlockSpec(memory_space=pltpu.VMEM)
    return pl.pallas_call(
        functools.partial(gather_kernel, counts),
        in_specs=[vmem] * len(blocks),
        out_specs=[vmem] * len(groups),
        out_shape=[jax.ShapeDtypeStruct((n * rows, width), BF16) for n in counts],
        compiler_params=pltpu.CompilerParams(vmem_limit_bytes=4 * 1024 * 1024),
        cost_estimate=pl.CostEstimate(
            flops=2 * 10**10, bytes_accessed=4 * 10**7, transcendentals=0
        ),
        name="gather_blocks",
    )(*blocks)


WINDOWS = (
    (0, (0, 1, 2)),
    (128, (3, 4)),
    (256, (5, 6)),
    (384, (7,)),
    (512, (8,)),
    (640, (9, 10, 11)),
    (768, (12,)),
    (896, (13, 14, 15)),
)


def split_stats(stats, lane):
    high = stats.astype(BF16)
    rest = stats - high.astype(F32)
    middle = rest.astype(BF16)
    low = (rest - middle.astype(F32)).astype(BF16)
    split = lane // HEADS
    packed = jnp.where(split == 2, low.astype(F32), 0.0)
    packed = jnp.where(split == 1, middle.astype(F32), packed)
    return jnp.where(split == 0, high.astype(F32), packed)


def attend_kernel(q_ref, *refs, fresh_ref=None):
    *keyval, out_ref = refs
    rows = q_ref.shape[0]
    scale = HEAD ** (-0.5)
    lane = lax.broadcasted_iota(jnp.int32, (rows, 256), 1)
    stat_lane = lax.broadcasted_iota(jnp.int32, (rows, STATS), 1)
    stats = jnp.zeros((rows, STATS), F32)
    blocks = [None] * (WIDTH // 128)

    def window(first):
        cols = slice(first, first + 256)
        pieces = [ref[:, cols] for ref in keyval]
        if fresh_ref is not None:
            n_own = fresh_ref.shape[0]
            own = fresh_ref[:, WIDTH + first : WIDTH + first + 256]
            pieces[0:1] = [own, keyval[0][n_own:, cols]]
        return jnp.concatenate(pieces, axis=0)

    def inside(start, head):
        first = head * HEAD - start
        return (lane >= first) & (lane < first + HEAD)

    for part in (WINDOWS[:4], WINDOWS[4:]):
        scores = []
        for start, heads in part:
            query = q_ref[:, start : start + 256]
            zero = jnp.zeros((), BF16)
            stack = [jnp.where(inside(start, head), query, zero) for head in heads]
            scores.append(
                lax.dot_general(
                    jnp.concatenate(stack, axis=0),
                    window(start),
                    (((1,), (1,)), ((), ())),
                    preferred_element_type=F32,
                )
            )
        tops = [jnp.max(s, axis=-1, keepdims=True) for s in scores]
        expos = [jnp.exp((s - t) * scale) for s, t in zip(scores, tops)]
        totals = [jnp.sum(e, axis=-1, keepdims=True) for e in expos]
        for (start, heads), top, expo, total in zip(part, tops, expos, totals):
            value = jnp.dot(
                expo.astype(BF16),
                window(WIDTH + start),
                preferred_element_type=F32,
            )
            value = value * (1.0 / total)
            stat = top * scale + jnp.log(total)
            for n, head in enumerate(heads):
                mine = slice(n * rows, (n + 1) * rows)
                picked = jnp.where(inside(start, head), value[mine], 0.0)
                for j in (0, 1):
                    block = start // 128 + j
                    piece = picked[:, 128 * j : 128 * j + 128]
                    blocks[block] = piece if blocks[block] is None else blocks[block] + piece
                stats = jnp.where(stat_lane % HEADS == head, stat[mine], stats)
    packed = split_stats(stats, stat_lane)
    for block, values in enumerate(blocks):
        out_ref[:, 128 * block : 128 * block + 128] = values.astype(BF16)
    out_ref[:, WIDTH:] = packed.astype(BF16)


def attend_cost(rows, keys):
    return pl.CostEstimate(
        flops=4 * HEADS * rows * keys * 256,
        bytes_accessed=4 * keys * WIDTH,
        transcendentals=HEADS * rows * keys,
    )


def attend(query, keyval):
    rows = query.shape[0]
    return pl.pallas_call(
        attend_kernel,
        in_specs=[pl.BlockSpec(memory_space=pltpu.VMEM)] * (1 + len(keyval)),
        out_specs=pl.BlockSpec(memory_space=pltpu.VMEM),
        out_shape=jax.ShapeDtypeStruct((rows, WIDTH + STATS), BF16),
        compiler_params=pltpu.CompilerParams(vmem_limit_bytes=VMEM_LIMIT),
        cost_estimate=attend_cost(rows, sum(x.shape[0] for x in keyval)),
        name="attend",
    )(query, *keyval)


def attend_own_kernel(
    q_ref, kv0, kv1, kv2, kv3, fresh_ref, time_ref, latent_ref, out_ref, base_ref, gain_ref
):
    image = lax.axis_index("guide")
    now = jnp.full(latent_ref.shape, time_ref[image // 2], jnp.int32)
    bar_now = alpha_bar(now)
    bar_prev = alpha_bar(now - STRIDE)
    latent_gain = jnp.sqrt(bar_prev) / jnp.sqrt(bar_now)
    noise_gain = jnp.sqrt(1.0 - bar_prev) - latent_gain * jnp.sqrt(1.0 - bar_now)
    is_cond = jnp.full(latent_ref.shape, image % 2, jnp.int32) == 0
    base_ref[...] = latent_gain * latent_ref[...]
    gain_ref[0] = noise_gain * jnp.where(is_cond, 4.5, -3.5)
    gain_ref[1] = noise_gain * jnp.where(is_cond, -3.5, 4.5)
    attend_kernel(q_ref, kv0, kv1, kv2, kv3, out_ref, fresh_ref=fresh_ref)


def attend_own(query, keyval, fresh, timestep, latent):
    rows = query.shape[0]
    vmem = pl.BlockSpec(memory_space=pltpu.VMEM)
    return pl.pallas_call(
        attend_own_kernel,
        in_specs=[vmem] * 6 + [pl.BlockSpec(memory_space=pltpu.SMEM), vmem],
        out_specs=[vmem] * 3,
        out_shape=[
            jax.ShapeDtypeStruct((rows, WIDTH + STATS), BF16),
            jax.ShapeDtypeStruct(latent.shape, F32),
            jax.ShapeDtypeStruct((2, *latent.shape), F32),
        ],
        compiler_params=pltpu.CompilerParams(vmem_limit_bytes=VMEM_LIMIT),
        cost_estimate=attend_cost(rows, sum(x.shape[0] for x in keyval)),
        name="attend_own",
    )(query, *keyval, fresh, timestep, latent)


def post_kernel(
    p0, p1, p2, p3, hidden_ref, mod_ref, w_out_ref, w_final_ref, scaled_ref, gain_ref,
    pick_ref, noise_ref, base_ref,
):
    pick = pick_ref[...]
    parts = (p0, p1, p2, p3)
    sums = [jnp.dot(p[:, WIDTH:], pick, preferred_element_type=F32) for p in parts]
    top = functools.reduce(jnp.maximum, sums)
    weights = [jnp.exp(s - top) for s in sums]
    total = functools.reduce(jnp.add, weights)
    mix = functools.reduce(
        jnp.add, [w * p[:, :WIDTH].astype(F32) for w, p in zip(weights, parts)]
    )
    attended = (mix / total).astype(BF16)
    source = hidden_ref[...].astype(F32)
    mixed = source + mod_ref[2] * jnp.dot(
        attended, w_out_ref[...], preferred_element_type=F32
    )
    final_in = (layer_norm(mixed) * (1.0 + mod_ref[4]) + mod_ref[3]).astype(BF16)
    w_wide = jnp.concatenate([w_final_ref[...]] * 8, axis=0)
    wide = lax.dot_general(
        final_in, w_wide, (((1,), (1,)), ((), ())), preferred_element_type=F32
    )
    rows = wide.shape[0]
    token = lax.broadcasted_iota(jnp.int32, wide.shape, 0) % 8
    place = lax.broadcasted_iota(jnp.int32, wide.shape, 1) // 16
    wide = jnp.where(token == place, wide, 0.0)
    noise = jnp.sum(wide.reshape(rows // 8, 8, 128), axis=1)
    noise_ref[...] = noise
    base_ref[...] = scaled_ref[...] + gain_ref[0] * noise


def post(parts, hidden, mod, w_out, w_final_t, scaled, gain, pick):
    rows = parts[0].shape[0]
    return pl.pallas_call(
        post_kernel,
        in_specs=[pl.BlockSpec(memory_space=pltpu.VMEM)] * 11,
        out_specs=[pl.BlockSpec(memory_space=pltpu.VMEM)] * 2,
        out_shape=[jax.ShapeDtypeStruct(scaled.shape, F32)] * 2,
        compiler_params=pltpu.CompilerParams(vmem_limit_bytes=VMEM_LIMIT),
        cost_estimate=pl.CostEstimate(
            flops=2 * rows * WIDTH * WIDTH, bytes_accessed=2 * WIDTH * WIDTH, transcendentals=0
        ),
        name="post",
    )(*parts, hidden, mod, w_out, w_final_t, scaled, gain, pick)


def body(hidden_in, stale_in, modulation, latent, timestep, w_qkv, w_out, w_final):
    hidden, stale = hidden_in[0], stale_in[0]
    mod = jnp.transpose(modulation, (1, 0, 2))
    rows = hidden.shape[0]

    stale, pick = lax.optimization_barrier((stale, head_selector()))
    stale_1, stale_2, stale_3 = [send(stale, z_xor(mask)) for mask in (1, 2, 3)]
    fresh = project_fresh(hidden, mod, w_qkv)
    query = fresh[:, :WIDTH]
    query_far, query_up, query_down = [send(query, y_shift(step)) for step in (2, 1, -1)]

    early = project_stale([stale, stale_1], w_qkv, 1)
    early_other = send(early, other_core)
    queries, blocks = gather_blocks((query_far, query_up, query_down), (stale_2, stale_3))
    blocks, early_other = lax.optimization_barrier((blocks, early_other))
    late = project_stale([blocks], w_qkv, 1)
    late_other = send(late, other_core)
    keyval = (early, late, early_other, late_other)

    partial = attend(queries, keyval)
    back = [
        send(partial[n * rows : (n + 1) * rows], y_shift(step))
        for n, step in enumerate((-2, -1, 1))
    ]
    own, scaled, gain = attend_own(query, keyval, fresh, timestep, latent[0])
    noise, base = post([own] + back, hidden, mod, w_out, w_final.T, scaled, gain, pick)
    partner = lax.ppermute(
        noise, "guide", [(i, i ^ 1) for i in range(lax.axis_size("guide"))]
    )
    return (base + gain[1] * partner)[None]


def solution(mesh):
    in_specs = (
        P("guide", "patch", None),
        P("guide", "patch", None),
        P("guide", None, None),
        P("guide", "patch", None),
        P(),
        P(),
        P(),
        P(),
    )
    out_specs = P("guide", "patch", None)
    return jax.shard_map(body, mesh=mesh, in_specs=in_specs, out_specs=out_specs, check_vma=False)
```

```python
import functools
import math

import jax
import jax.numpy as jnp
from jax import lax
from jax.experimental import pallas as pl
from jax.experimental.pallas import tpu as pltpu
from jax.sharding import PartitionSpec as P

HEADS = 16
HEAD = 72
WIDTH = 1152
STRIDE = 50
NY, NZ, NC = 4, 4, 2
STATS = 128
CHUNK = 384
LOG2_E = 1.4426950408889634
BF16, F32 = jnp.bfloat16, jnp.float32
VMEM_LIMIT = 32 * 1024 * 1024


def layer_norm(values):
    mean = jnp.mean(values, axis=-1, keepdims=True)
    centred = values - mean
    var = jnp.mean(centred * centred, axis=-1, keepdims=True)
    return centred / jnp.sqrt(var + 1e-06)


def alpha_bar(step_index):
    angle = (step_index.astype(F32) / 1000.0 + 0.008) / 1.008 * (math.pi / 2.0)
    return jnp.cos(angle) ** 2


def send(value, route):
    pairs = []
    for y in range(NY):
        for z in range(NZ):
            for c in range(NC):
                ty, tz, tc = route(y, z, c)
                pairs.append(((y * NZ + z) * NC + c, ((ty % NY) * NZ + tz) * NC + tc))
    return lax.ppermute(value, "patch", pairs)


def z_xor(mask):
    return lambda y, z, c: (y, z ^ mask, c)


def other_core(y, z, c):
    return y, z, c ^ 1


def y_shift(step):
    return lambda y, z, c: (y + step, z, c)


def selector_kernel(out_ref):
    row = lax.broadcasted_iota(jnp.int32, (STATS, WIDTH), 0)
    col = lax.broadcasted_iota(jnp.int32, (STATS, WIDTH), 1)
    offset = col - (row % HEADS) * HEAD
    pick = (row < 3 * HEADS) & (offset >= 0) & (offset < HEAD)
    out_ref[...] = jnp.where(pick, 1.0, 0.0).astype(BF16)


def head_selector():
    return pl.pallas_call(
        selector_kernel,
        out_specs=pl.BlockSpec(memory_space=pltpu.VMEM),
        out_shape=jax.ShapeDtypeStruct((STATS, WIDTH), BF16),
        compiler_params=pltpu.CompilerParams(vmem_limit_bytes=4 * 1024 * 1024),
        cost_estimate=pl.CostEstimate(
            flops=2 * 10**10, bytes_accessed=4 * 10**7, transcendentals=0
        ),
        name="head_selector",
    )()


def fresh_kernel(hidden_ref, mod_ref, w_ref, out_ref):
    source = hidden_ref[...].astype(F32)
    attn_in = (layer_norm(source) * (1.0 + mod_ref[1]) + mod_ref[0]).astype(BF16)
    for start in range(0, w_ref.shape[1], CHUNK):
        out_ref[:, start : start + CHUNK] = jnp.dot(
            attn_in, w_ref[:, start : start + CHUNK], preferred_element_type=F32
        ).astype(BF16)


def project_fresh(hidden, mod, w_qkv):
    rows, width = hidden.shape
    cols = w_qkv.shape[1]
    return pl.pallas_call(
        fresh_kernel,
        in_specs=[pl.BlockSpec(memory_space=pltpu.VMEM)] * 3,
        out_specs=pl.BlockSpec(memory_space=pltpu.VMEM),
        out_shape=jax.ShapeDtypeStruct((rows, cols), BF16),
        compiler_params=pltpu.CompilerParams(vmem_limit_bytes=VMEM_LIMIT),
        cost_estimate=pl.CostEstimate(
            flops=2 * rows * width * cols, bytes_accessed=2 * width * cols, transcendentals=0
        ),
        name="fresh_qkv",
    )(hidden, mod, w_qkv)


def stale_kernel(*refs):
    *blocks, w_ref, out_ref = refs
    keys = jnp.concatenate([x[...] for x in blocks], axis=0)
    for start in range(0, out_ref.shape[1], CHUNK):
        out_ref[:, start : start + CHUNK] = jnp.dot(
            keys,
            w_ref[:, WIDTH + start : WIDTH + start + CHUNK],
            preferred_element_type=F32,
        ).astype(BF16)


def project_stale(blocks, w_qkv, flops):
    rows = len(blocks) * blocks[0].shape[0]
    width, cols = w_qkv.shape
    cols -= width
    return pl.pallas_call(
        stale_kernel,
        in_specs=[pl.BlockSpec(memory_space=pltpu.VMEM)] * (len(blocks) + 1),
        out_specs=pl.BlockSpec(memory_space=pltpu.VMEM),
        out_shape=jax.ShapeDtypeStruct((rows, cols), BF16),
        compiler_params=pltpu.CompilerParams(vmem_limit_bytes=VMEM_LIMIT),
        cost_estimate=pl.CostEstimate(
            flops=flops, bytes_accessed=1, transcendentals=0
        ),
        name="stale_kv",
    )(*blocks, w_qkv)


def gather_kernel(counts, *refs):
    first = 0
    for out_ref, count in zip(refs[sum(counts) :], counts):
        for n in range(count):
            block = refs[first + n]
            rows = block.shape[0]
            out_ref[n * rows : (n + 1) * rows, :] = block[...]
        first += count


def gather_blocks(*groups):
    blocks = [block for group in groups for block in group]
    rows, width = blocks[0].shape
    counts = tuple(len(group) for group in groups)
    vmem = pl.BlockSpec(memory_space=pltpu.VMEM)
    return pl.pallas_call(
        functools.partial(gather_kernel, counts),
        in_specs=[vmem] * len(blocks),
        out_specs=[vmem] * len(groups),
        out_shape=[jax.ShapeDtypeStruct((n * rows, width), BF16) for n in counts],
        compiler_params=pltpu.CompilerParams(vmem_limit_bytes=4 * 1024 * 1024),
        cost_estimate=pl.CostEstimate(
            flops=2 * 10**10, bytes_accessed=4 * 10**7, transcendentals=0
        ),
        name="gather_blocks",
    )(*blocks)


WINDOWS = (
    (0, (0, 1, 2)),
    (128, (3, 4)),
    (256, (5, 6)),
    (384, (7,)),
    (512, (8,)),
    (640, (9, 10, 11)),
    (768, (12,)),
    (896, (13, 14, 15)),
)


def split_stats(stats, lane):
    high = stats.astype(BF16)
    rest = stats - high.astype(F32)
    middle = rest.astype(BF16)
    low = (rest - middle.astype(F32)).astype(BF16)
    split = lane // HEADS
    packed = jnp.where(split == 2, low.astype(F32), 0.0)
    packed = jnp.where(split == 1, middle.astype(F32), packed)
    return jnp.where(split == 0, high.astype(F32), packed)


def attend_kernel(q_ref, *refs, fresh_ref=None):
    *keyval, out_ref = refs
    rows = q_ref.shape[0]
    scale = HEAD ** (-0.5)
    lane = lax.broadcasted_iota(jnp.int32, (rows, 256), 1)
    stat_lane = lax.broadcasted_iota(jnp.int32, (rows, STATS), 1)
    stats = jnp.zeros((rows, STATS), F32)
    blocks = [None] * (WIDTH // 128)

    def window(first):
        cols = slice(first, first + 256)
        pieces = [ref[:, cols] for ref in keyval]
        if fresh_ref is not None:
            n_own = fresh_ref.shape[0]
            own = fresh_ref[:, WIDTH + first : WIDTH + first + 256]
            pieces[0:1] = [own, keyval[0][n_own:, cols]]
        return jnp.concatenate(pieces, axis=0)

    def inside(start, head):
        first = head * HEAD - start
        return (lane >= first) & (lane < first + HEAD)

    for part in (WINDOWS,):
        scores = []
        for start, heads in part:
            query = q_ref[:, start : start + 256]
            zero = jnp.zeros((), BF16)
            stack = [jnp.where(inside(start, head), query, zero) for head in heads]
            scores.append(
                lax.dot_general(
                    jnp.concatenate(stack, axis=0),
                    window(start),
                    (((1,), (1,)), ((), ())),
                    preferred_element_type=F32,
                )
            )
        tops = [jnp.max(s, axis=-1, keepdims=True) for s in scores]
        expos = [jnp.exp2((s - t) * (scale * LOG2_E)) for s, t in zip(scores, tops)]
        totals = [jnp.sum(e, axis=-1, keepdims=True) for e in expos]
        for (start, heads), top, expo, total in zip(part, tops, expos, totals):
            value = jnp.dot(
                expo.astype(BF16),
                window(WIDTH + start),
                preferred_element_type=F32,
            )
            value = value * (1.0 / total)
            stat = top * scale + jnp.log(total)
            for n, head in enumerate(heads):
                mine = slice(n * rows, (n + 1) * rows)
                picked = jnp.where(inside(start, head), value[mine], 0.0)
                for j in (0, 1):
                    block = start // 128 + j
                    piece = picked[:, 128 * j : 128 * j + 128]
                    blocks[block] = piece if blocks[block] is None else blocks[block] + piece
                stats = jnp.where(stat_lane % HEADS == head, stat[mine], stats)
    packed = split_stats(stats, stat_lane)
    for block, values in enumerate(blocks):
        out_ref[:, 128 * block : 128 * block + 128] = values.astype(BF16)
    out_ref[:, WIDTH:] = packed.astype(BF16)


def attend_cost(rows, keys):
    return pl.CostEstimate(
        flops=4 * HEADS * rows * keys * 256,
        bytes_accessed=4 * keys * WIDTH,
        transcendentals=HEADS * rows * keys,
    )


def attend(query, keyval):
    rows = query.shape[0]
    return pl.pallas_call(
        attend_kernel,
        in_specs=[pl.BlockSpec(memory_space=pltpu.VMEM)] * (1 + len(keyval)),
        out_specs=pl.BlockSpec(memory_space=pltpu.VMEM),
        out_shape=jax.ShapeDtypeStruct((rows, WIDTH + STATS), BF16),
        compiler_params=pltpu.CompilerParams(vmem_limit_bytes=VMEM_LIMIT),
        cost_estimate=attend_cost(rows, sum(x.shape[0] for x in keyval)),
        name="attend",
    )(query, *keyval)


def attend_own_kernel(
    q_ref, kv0, kv1, kv2, kv3, fresh_ref, time_ref, latent_ref, out_ref, base_ref, gain_ref
):
    image = lax.axis_index("guide")
    now = jnp.full(latent_ref.shape, time_ref[image // 2], jnp.int32)
    bar_now = alpha_bar(now)
    bar_prev = alpha_bar(now - STRIDE)
    latent_gain = jnp.sqrt(bar_prev) / jnp.sqrt(bar_now)
    noise_gain = jnp.sqrt(1.0 - bar_prev) - latent_gain * jnp.sqrt(1.0 - bar_now)
    is_cond = jnp.full(latent_ref.shape, image % 2, jnp.int32) == 0
    base_ref[...] = latent_gain * latent_ref[...]
    gain_ref[0] = noise_gain * jnp.where(is_cond, 4.5, -3.5)
    gain_ref[1] = noise_gain * jnp.where(is_cond, -3.5, 4.5)
    attend_kernel(q_ref, kv0, kv1, kv2, kv3, out_ref, fresh_ref=fresh_ref)


def attend_own(query, keyval, fresh, timestep, latent):
    rows = query.shape[0]
    vmem = pl.BlockSpec(memory_space=pltpu.VMEM)
    return pl.pallas_call(
        attend_own_kernel,
        in_specs=[vmem] * 6 + [pl.BlockSpec(memory_space=pltpu.SMEM), vmem],
        out_specs=[vmem] * 3,
        out_shape=[
            jax.ShapeDtypeStruct((rows, WIDTH + STATS), BF16),
            jax.ShapeDtypeStruct(latent.shape, F32),
            jax.ShapeDtypeStruct((2, *latent.shape), F32),
        ],
        compiler_params=pltpu.CompilerParams(vmem_limit_bytes=VMEM_LIMIT),
        cost_estimate=attend_cost(rows, sum(x.shape[0] for x in keyval)),
        name="attend_own",
    )(query, *keyval, fresh, timestep, latent)


def post_kernel(
    p0, p1, p2, p3, hidden_ref, mod_ref, w_out_ref, w_final_ref, scaled_ref, gain_ref,
    pick_ref, noise_ref, base_ref,
):
    pick = pick_ref[...]
    parts = (p0, p1, p2, p3)
    sums = [jnp.dot(p[:, WIDTH:], pick, preferred_element_type=F32) for p in parts]
    top = functools.reduce(jnp.maximum, sums)
    weights = [jnp.exp(s - top) for s in sums]
    total = functools.reduce(jnp.add, weights)
    mix = functools.reduce(
        jnp.add, [w * p[:, :WIDTH].astype(F32) for w, p in zip(weights, parts)]
    )
    attended = (mix / total).astype(BF16)
    source = hidden_ref[...].astype(F32)
    mixed = source + mod_ref[2] * jnp.dot(
        attended, w_out_ref[...], preferred_element_type=F32
    )
    final_in = (layer_norm(mixed) * (1.0 + mod_ref[4]) + mod_ref[3]).astype(BF16)
    w_wide = jnp.concatenate([w_final_ref[...]] * 8, axis=0)
    wide = lax.dot_general(
        final_in, w_wide, (((1,), (1,)), ((), ())), preferred_element_type=F32
    )
    rows = wide.shape[0]
    token = lax.broadcasted_iota(jnp.int32, wide.shape, 0) % 8
    place = lax.broadcasted_iota(jnp.int32, wide.shape, 1) // 16
    wide = jnp.where(token == place, wide, 0.0)
    noise = jnp.sum(wide.reshape(rows // 8, 8, 128), axis=1)
    noise_ref[...] = noise
    base_ref[...] = scaled_ref[...] + gain_ref[0] * noise


def post(parts, hidden, mod, w_out, w_final_t, scaled, gain, pick):
    rows = parts[0].shape[0]
    return pl.pallas_call(
        post_kernel,
        in_specs=[pl.BlockSpec(memory_space=pltpu.VMEM)] * 11,
        out_specs=[pl.BlockSpec(memory_space=pltpu.VMEM)] * 2,
        out_shape=[jax.ShapeDtypeStruct(scaled.shape, F32)] * 2,
        compiler_params=pltpu.CompilerParams(vmem_limit_bytes=VMEM_LIMIT),
        cost_estimate=pl.CostEstimate(
            flops=2 * rows * WIDTH * WIDTH, bytes_accessed=2 * WIDTH * WIDTH, transcendentals=0
        ),
        name="post",
    )(*parts, hidden, mod, w_out, w_final_t, scaled, gain, pick)


def body(hidden_in, stale_in, modulation, latent, timestep, w_qkv, w_out, w_final):
    hidden, stale = hidden_in[0], stale_in[0]
    mod = jnp.transpose(modulation, (1, 0, 2))
    rows = hidden.shape[0]

    stale, pick = lax.optimization_barrier((stale, head_selector()))
    stale_1, stale_2, stale_3 = [send(stale, z_xor(mask)) for mask in (1, 2, 3)]
    fresh = project_fresh(hidden, mod, w_qkv)
    query = fresh[:, :WIDTH]
    query_up, query_down, query_far = [send(query, y_shift(step)) for step in (1, -1, 2)]

    early = project_stale([stale, stale_1], w_qkv, 1)
    early_other = send(early, other_core)
    queries, blocks = gather_blocks((query_up, query_down, query_far), (stale_2, stale_3))
    blocks, early_other = lax.optimization_barrier((blocks, early_other))
    late = project_stale([blocks], w_qkv, 1)
    late_other = send(late, other_core)
    keyval = (early, late, early_other, late_other)

    partial = attend(queries, keyval)
    back = [
        send(partial[n * rows : (n + 1) * rows], y_shift(step))
        for n, step in enumerate((-1, 1, -2))
    ]
    own, scaled, gain = attend_own(query, keyval, fresh, timestep, latent[0])
    noise, base = post([own] + back, hidden, mod, w_out, w_final.T, scaled, gain, pick)
    partner = lax.ppermute(
        noise, "guide", [(i, i ^ 1) for i in range(lax.axis_size("guide"))]
    )
    return (base + gain[1] * partner)[None]


def solution(mesh):
    in_specs = (
        P("guide", "patch", None),
        P("guide", "patch", None),
        P("guide", None, None),
        P("guide", "patch", None),
        P(),
        P(),
        P(),
        P(),
    )
    out_specs = P("guide", "patch", None)
    return jax.shard_map(body, mesh=mesh, in_specs=in_specs, out_specs=out_specs, check_vma=False)
```

```python
import functools
import math

import jax
import jax.numpy as jnp
from jax import lax
from jax.experimental import pallas as pl
from jax.experimental.pallas import tpu as pltpu
from jax.sharding import PartitionSpec as P

HEADS = 16
HEAD = 72
WIDTH = 1152
STRIDE = 50
NY, NZ, NC = 4, 4, 2
STATS = 128
CHUNK = 384
LOG2_E = 1.4426950408889634
BF16, F32 = jnp.bfloat16, jnp.float32
VMEM_LIMIT = 32 * 1024 * 1024


def layer_norm(values):
    mean = jnp.mean(values, axis=-1, keepdims=True)
    centred = values - mean
    var = jnp.mean(centred * centred, axis=-1, keepdims=True)
    return centred / jnp.sqrt(var + 1e-06)


def alpha_bar(step_index):
    angle = (step_index.astype(F32) / 1000.0 + 0.008) / 1.008 * (math.pi / 2.0)
    return jnp.cos(angle) ** 2


def send(value, route):
    pairs = []
    for y in range(NY):
        for z in range(NZ):
            for c in range(NC):
                ty, tz, tc = route(y, z, c)
                pairs.append(((y * NZ + z) * NC + c, ((ty % NY) * NZ + tz) * NC + tc))
    return lax.ppermute(value, "patch", pairs)


def z_xor(mask):
    return lambda y, z, c: (y, z ^ mask, c)


def other_core(y, z, c):
    return y, z, c ^ 1


def y_shift(step):
    return lambda y, z, c: (y + step, z, c)


def selector_kernel(out_ref):
    row = lax.broadcasted_iota(jnp.int32, (STATS, WIDTH), 0)
    col = lax.broadcasted_iota(jnp.int32, (STATS, WIDTH), 1)
    offset = col - (row % HEADS) * HEAD
    pick = (row < 3 * HEADS) & (offset >= 0) & (offset < HEAD)
    out_ref[...] = jnp.where(pick, 1.0, 0.0).astype(BF16)


def head_selector():
    return pl.pallas_call(
        selector_kernel,
        out_specs=pl.BlockSpec(memory_space=pltpu.VMEM),
        out_shape=jax.ShapeDtypeStruct((STATS, WIDTH), BF16),
        compiler_params=pltpu.CompilerParams(vmem_limit_bytes=4 * 1024 * 1024),
        cost_estimate=pl.CostEstimate(
            flops=2 * 10**10, bytes_accessed=4 * 10**7, transcendentals=0
        ),
        name="head_selector",
    )()


def fresh_kernel(hidden_ref, mod_ref, w_ref, out_ref):
    source = hidden_ref[...].astype(F32)
    attn_in = (layer_norm(source) * (1.0 + mod_ref[1]) + mod_ref[0]).astype(BF16)
    for start in range(0, w_ref.shape[1], CHUNK):
        out_ref[:, start : start + CHUNK] = jnp.dot(
            attn_in, w_ref[:, start : start + CHUNK], preferred_element_type=F32
        ).astype(BF16)


def project_fresh(hidden, mod, w_qkv):
    rows, width = hidden.shape
    cols = w_qkv.shape[1]
    return pl.pallas_call(
        fresh_kernel,
        in_specs=[pl.BlockSpec(memory_space=pltpu.VMEM)] * 3,
        out_specs=pl.BlockSpec(memory_space=pltpu.VMEM),
        out_shape=jax.ShapeDtypeStruct((rows, cols), BF16),
        compiler_params=pltpu.CompilerParams(vmem_limit_bytes=VMEM_LIMIT),
        cost_estimate=pl.CostEstimate(
            flops=2 * rows * width * cols, bytes_accessed=2 * width * cols, transcendentals=0
        ),
        name="fresh_qkv",
    )(hidden, mod, w_qkv)


def stale_kernel(*refs):
    *blocks, w_ref, out_ref = refs
    keys = jnp.concatenate([x[...] for x in blocks], axis=0)
    for start in range(0, out_ref.shape[1], CHUNK):
        out_ref[:, start : start + CHUNK] = jnp.dot(
            keys,
            w_ref[:, WIDTH + start : WIDTH + start + CHUNK],
            preferred_element_type=F32,
        ).astype(BF16)


def project_stale(blocks, w_qkv, flops):
    rows = len(blocks) * blocks[0].shape[0]
    width, cols = w_qkv.shape
    cols -= width
    return pl.pallas_call(
        stale_kernel,
        in_specs=[pl.BlockSpec(memory_space=pltpu.VMEM)] * (len(blocks) + 1),
        out_specs=pl.BlockSpec(memory_space=pltpu.VMEM),
        out_shape=jax.ShapeDtypeStruct((rows, cols), BF16),
        compiler_params=pltpu.CompilerParams(vmem_limit_bytes=VMEM_LIMIT),
        cost_estimate=pl.CostEstimate(
            flops=flops, bytes_accessed=1, transcendentals=0
        ),
        name="stale_kv",
    )(*blocks, w_qkv)


def gather_kernel(counts, *refs):
    first = 0
    for out_ref, count in zip(refs[sum(counts) :], counts):
        for n in range(count):
            block = refs[first + n]
            rows = block.shape[0]
            out_ref[n * rows : (n + 1) * rows, :] = block[...]
        first += count


def gather_blocks(*groups):
    blocks = [block for group in groups for block in group]
    rows, width = blocks[0].shape
    counts = tuple(len(group) for group in groups)
    vmem = pl.BlockSpec(memory_space=pltpu.VMEM)
    return pl.pallas_call(
        functools.partial(gather_kernel, counts),
        in_specs=[vmem] * len(blocks),
        out_specs=[vmem] * len(groups),
        out_shape=[jax.ShapeDtypeStruct((n * rows, width), BF16) for n in counts],
        compiler_params=pltpu.CompilerParams(vmem_limit_bytes=4 * 1024 * 1024),
        cost_estimate=pl.CostEstimate(
            flops=2 * 10**10, bytes_accessed=4 * 10**7, transcendentals=0
        ),
        name="gather_blocks",
    )(*blocks)


WINDOWS = (
    (0, (0, 1, 2)),
    (128, (3, 4)),
    (256, (5, 6)),
    (384, (7,)),
    (512, (8,)),
    (640, (9, 10, 11)),
    (768, (12,)),
    (896, (13, 14, 15)),
)


def split_stats(stats, lane):
    high = stats.astype(BF16)
    rest = stats - high.astype(F32)
    middle = rest.astype(BF16)
    low = (rest - middle.astype(F32)).astype(BF16)
    split = lane // HEADS
    packed = jnp.where(split == 2, low.astype(F32), 0.0)
    packed = jnp.where(split == 1, middle.astype(F32), packed)
    return jnp.where(split == 0, high.astype(F32), packed)


def attend_kernel(q_ref, *refs, fresh_ref=None):
    *keyval, out_ref = refs
    rows = q_ref.shape[0]
    scale = HEAD ** (-0.5)
    lane = lax.broadcasted_iota(jnp.int32, (rows, 256), 1)
    stat_lane = lax.broadcasted_iota(jnp.int32, (rows, STATS), 1)
    stats = jnp.zeros((rows, STATS), F32)
    blocks = [None] * (WIDTH // 128)

    def window(first):
        cols = slice(first, first + 256)
        pieces = [ref[:, cols] for ref in keyval]
        if fresh_ref is not None:
            n_own = fresh_ref.shape[0]
            own = fresh_ref[:, WIDTH + first : WIDTH + first + 256]
            pieces[0:1] = [own, keyval[0][n_own:, cols]]
        return jnp.concatenate(pieces, axis=0)

    def inside(start, head):
        first = head * HEAD - start
        return (lane >= first) & (lane < first + HEAD)

    for part in (WINDOWS,):
        scores = []
        for start, heads in part:
            query = q_ref[:, start : start + 256]
            zero = jnp.zeros((), BF16)
            stack = [jnp.where(inside(start, head), query, zero) for head in heads]
            scores.append(
                lax.dot_general(
                    jnp.concatenate(stack, axis=0),
                    window(start),
                    (((1,), (1,)), ((), ())),
                    preferred_element_type=F32,
                )
            )
        tops = [jnp.max(s, axis=-1, keepdims=True) for s in scores]
        expos = [jnp.exp2((s - t) * (scale * LOG2_E)) for s, t in zip(scores, tops)]
        totals = [jnp.sum(e, axis=-1, keepdims=True) for e in expos]
        for (start, heads), top, expo, total in zip(part, tops, expos, totals):
            value = jnp.dot(
                expo.astype(BF16),
                window(WIDTH + start),
                preferred_element_type=F32,
            )
            value = value * (1.0 / total)
            stat = top * scale + jnp.log(total)
            for n, head in enumerate(heads):
                mine = slice(n * rows, (n + 1) * rows)
                picked = jnp.where(inside(start, head), value[mine], 0.0)
                for j in (0, 1):
                    block = start // 128 + j
                    piece = picked[:, 128 * j : 128 * j + 128]
                    blocks[block] = piece if blocks[block] is None else blocks[block] + piece
                stats = jnp.where(stat_lane % HEADS == head, stat[mine], stats)
    packed = split_stats(stats, stat_lane)
    for block, values in enumerate(blocks):
        out_ref[:, 128 * block : 128 * block + 128] = values.astype(BF16)
    out_ref[:, WIDTH:] = packed.astype(BF16)


def attend_cost(rows, keys):
    return pl.CostEstimate(
        flops=4 * HEADS * rows * keys * 256,
        bytes_accessed=4 * keys * WIDTH,
        transcendentals=HEADS * rows * keys,
    )


def attend(query, keyval):
    rows = query.shape[0]
    return pl.pallas_call(
        attend_kernel,
        in_specs=[pl.BlockSpec(memory_space=pltpu.VMEM)] * (1 + len(keyval)),
        out_specs=pl.BlockSpec(memory_space=pltpu.VMEM),
        out_shape=jax.ShapeDtypeStruct((rows, WIDTH + STATS), BF16),
        compiler_params=pltpu.CompilerParams(vmem_limit_bytes=VMEM_LIMIT),
        cost_estimate=attend_cost(rows, sum(x.shape[0] for x in keyval)),
        name="attend",
    )(query, *keyval)


def attend_own_kernel(
    q_ref, kv0, kv1, kv2, kv3, fresh_ref, time_ref, latent_ref, out_ref, base_ref, gain_ref
):
    image = lax.axis_index("guide")
    now = jnp.full(latent_ref.shape, time_ref[image // 2], jnp.int32)
    bar_now = alpha_bar(now)
    bar_prev = alpha_bar(now - STRIDE)
    latent_gain = jnp.sqrt(bar_prev) / jnp.sqrt(bar_now)
    noise_gain = jnp.sqrt(1.0 - bar_prev) - latent_gain * jnp.sqrt(1.0 - bar_now)
    is_cond = jnp.full(latent_ref.shape, image % 2, jnp.int32) == 0
    base_ref[...] = latent_gain * latent_ref[...]
    gain_ref[0] = noise_gain * jnp.where(is_cond, 4.5, -3.5)
    gain_ref[1] = noise_gain * jnp.where(is_cond, -3.5, 4.5)
    attend_kernel(q_ref, kv0, kv1, kv2, kv3, out_ref, fresh_ref=fresh_ref)


def attend_own(query, keyval, fresh, timestep, latent):
    rows = query.shape[0]
    vmem = pl.BlockSpec(memory_space=pltpu.VMEM)
    return pl.pallas_call(
        attend_own_kernel,
        in_specs=[vmem] * 6 + [pl.BlockSpec(memory_space=pltpu.SMEM), vmem],
        out_specs=[vmem] * 3,
        out_shape=[
            jax.ShapeDtypeStruct((rows, WIDTH + STATS), BF16),
            jax.ShapeDtypeStruct(latent.shape, F32),
            jax.ShapeDtypeStruct((2, *latent.shape), F32),
        ],
        compiler_params=pltpu.CompilerParams(vmem_limit_bytes=VMEM_LIMIT),
        cost_estimate=attend_cost(rows, sum(x.shape[0] for x in keyval)),
        name="attend_own",
    )(query, *keyval, fresh, timestep, latent)


def post_kernel(
    p0, p1, p2, p3, hidden_ref, mod_ref, w_out_ref, w_final_ref, scaled_ref, gain_ref,
    pick_ref, noise_ref, base_ref,
):
    pick = pick_ref[...]
    parts = (p0, p1, p2, p3)
    sums = [jnp.dot(p[:, WIDTH:], pick, preferred_element_type=F32) for p in parts]
    top = functools.reduce(jnp.maximum, sums)
    weights = [jnp.exp(s - top) for s in sums]
    total = functools.reduce(jnp.add, weights)
    mix = functools.reduce(
        jnp.add, [w * p[:, :WIDTH].astype(F32) for w, p in zip(weights, parts)]
    )
    attended = (mix / total).astype(BF16)
    source = hidden_ref[...].astype(F32)
    mixed = source + mod_ref[2] * jnp.dot(
        attended, w_out_ref[...], preferred_element_type=F32
    )
    final_in = (layer_norm(mixed) * (1.0 + mod_ref[4]) + mod_ref[3]).astype(BF16)
    w_wide = jnp.concatenate([w_final_ref[...]] * 8, axis=0)
    wide = lax.dot_general(
        final_in, w_wide, (((1,), (1,)), ((), ())), preferred_element_type=F32
    )
    rows = wide.shape[0]
    token = lax.broadcasted_iota(jnp.int32, wide.shape, 0) % 8
    place = lax.broadcasted_iota(jnp.int32, wide.shape, 1) // 16
    wide = jnp.where(token == place, wide, 0.0)
    noise = jnp.sum(wide.reshape(rows // 8, 8, 128), axis=1)
    noise_ref[...] = noise
    base_ref[...] = scaled_ref[...] + gain_ref[0] * noise


def post(parts, hidden, mod, w_out, w_final_t, scaled, gain, pick):
    rows = parts[0].shape[0]
    return pl.pallas_call(
        post_kernel,
        in_specs=[pl.BlockSpec(memory_space=pltpu.VMEM)] * 11,
        out_specs=[pl.BlockSpec(memory_space=pltpu.VMEM)] * 2,
        out_shape=[jax.ShapeDtypeStruct(scaled.shape, F32)] * 2,
        compiler_params=pltpu.CompilerParams(vmem_limit_bytes=VMEM_LIMIT),
        cost_estimate=pl.CostEstimate(
            flops=2 * rows * WIDTH * WIDTH, bytes_accessed=2 * WIDTH * WIDTH, transcendentals=0
        ),
        name="post",
    )(*parts, hidden, mod, w_out, w_final_t, scaled, gain, pick)


def body(hidden_in, stale_in, modulation, latent, timestep, w_qkv, w_out, w_final):
    hidden, stale = hidden_in[0], stale_in[0]
    mod = jnp.transpose(modulation, (1, 0, 2))
    rows = hidden.shape[0]

    sent, pick = lax.optimization_barrier((stale, head_selector()))
    stale_1 = send(stale, z_xor(1))
    stale_2, stale_3 = [send(sent, z_xor(mask)) for mask in (2, 3)]
    fresh = project_fresh(hidden, mod, w_qkv)
    query = fresh[:, :WIDTH]
    query_up, query_down, query_far = [send(query, y_shift(step)) for step in (1, -1, 2)]

    early = project_stale([stale, stale_1], w_qkv, 2 * 10**10)
    early_other = send(early, other_core)
    queries, blocks = gather_blocks((query_up, query_down, query_far), (stale_2, stale_3))
    blocks, early_other = lax.optimization_barrier((blocks, early_other))
    late = project_stale([blocks], w_qkv, 1)
    late_other = send(late, other_core)
    keyval = (early, late, early_other, late_other)

    partial = attend(queries, keyval)
    back = [
        send(partial[n * rows : (n + 1) * rows], y_shift(step))
        for n, step in enumerate((-1, 1, -2))
    ]
    own, scaled, gain = attend_own(query, keyval, fresh, timestep, latent[0])
    noise, base = post([own] + back, hidden, mod, w_out, w_final.T, scaled, gain, pick)
    partner = lax.ppermute(
        noise, "guide", [(i, i ^ 1) for i in range(lax.axis_size("guide"))]
    )
    return (base + gain[1] * partner)[None]


def solution(mesh):
    in_specs = (
        P("guide", "patch", None),
        P("guide", "patch", None),
        P("guide", None, None),
        P("guide", "patch", None),
        P(),
        P(),
        P(),
        P(),
    )
    out_specs = P("guide", "patch", None)
    return jax.shard_map(body, mesh=mesh, in_specs=in_specs, out_specs=out_specs, check_vma=False)
```

```python
import functools
import math

import jax
import jax.numpy as jnp
from jax import lax
from jax.experimental import pallas as pl
from jax.experimental.pallas import tpu as pltpu
from jax.sharding import PartitionSpec as P

HEADS = 16
HEAD = 72
WIDTH = 1152
STRIDE = 50
NY, NZ, NC = 4, 4, 2
STATS = 128
CHUNK = 384
LOG2_E = 1.4426950408889634
BF16, F32 = jnp.bfloat16, jnp.float32
VMEM_LIMIT = 32 * 1024 * 1024


def layer_norm(values):
    mean = jnp.mean(values, axis=-1, keepdims=True)
    centred = values - mean
    var = jnp.mean(centred * centred, axis=-1, keepdims=True)
    return centred / jnp.sqrt(var + 1e-06)


def alpha_bar(step_index):
    angle = (step_index.astype(F32) / 1000.0 + 0.008) / 1.008 * (math.pi / 2.0)
    return jnp.cos(angle) ** 2


def send(value, route):
    pairs = []
    for y in range(NY):
        for z in range(NZ):
            for c in range(NC):
                ty, tz, tc = route(y, z, c)
                pairs.append(((y * NZ + z) * NC + c, ((ty % NY) * NZ + tz) * NC + tc))
    return lax.ppermute(value, "patch", pairs)


def z_xor(mask):
    return lambda y, z, c: (y, z ^ mask, c)


def other_core(y, z, c):
    return y, z, c ^ 1


def y_shift(step):
    return lambda y, z, c: (y + step, z, c)


def selector_kernel(out_ref):
    row = lax.broadcasted_iota(jnp.int32, (STATS, WIDTH), 0)
    col = lax.broadcasted_iota(jnp.int32, (STATS, WIDTH), 1)
    offset = col - (row % HEADS) * HEAD
    pick = (row < 3 * HEADS) & (offset >= 0) & (offset < HEAD)
    out_ref[...] = jnp.where(pick, 1.0, 0.0).astype(BF16)


def head_selector():
    return pl.pallas_call(
        selector_kernel,
        out_specs=pl.BlockSpec(memory_space=pltpu.VMEM),
        out_shape=jax.ShapeDtypeStruct((STATS, WIDTH), BF16),
        compiler_params=pltpu.CompilerParams(vmem_limit_bytes=4 * 1024 * 1024),
        cost_estimate=pl.CostEstimate(
            flops=2 * 10**10, bytes_accessed=4 * 10**7, transcendentals=0
        ),
        name="head_selector",
    )()


def fresh_kernel(hidden_ref, mod_ref, w_ref, out_ref):
    source = hidden_ref[...].astype(F32)
    attn_in = (layer_norm(source) * (1.0 + mod_ref[1]) + mod_ref[0]).astype(BF16)
    for start in range(0, w_ref.shape[1], CHUNK):
        out_ref[:, start : start + CHUNK] = jnp.dot(
            attn_in, w_ref[:, start : start + CHUNK], preferred_element_type=F32
        ).astype(BF16)


def project_fresh(hidden, mod, w_qkv):
    rows, width = hidden.shape
    cols = w_qkv.shape[1]
    return pl.pallas_call(
        fresh_kernel,
        in_specs=[pl.BlockSpec(memory_space=pltpu.VMEM)] * 3,
        out_specs=pl.BlockSpec(memory_space=pltpu.VMEM),
        out_shape=jax.ShapeDtypeStruct((rows, cols), BF16),
        compiler_params=pltpu.CompilerParams(vmem_limit_bytes=VMEM_LIMIT),
        cost_estimate=pl.CostEstimate(
            flops=2 * rows * width * cols, bytes_accessed=2 * width * cols, transcendentals=0
        ),
        name="fresh_qkv",
    )(hidden, mod, w_qkv)


def stale_kernel(*refs):
    *blocks, w_ref, out_ref = refs
    keys = jnp.concatenate([x[...] for x in blocks], axis=0)
    for start in range(0, out_ref.shape[1], CHUNK):
        out_ref[:, start : start + CHUNK] = jnp.dot(
            keys,
            w_ref[:, WIDTH + start : WIDTH + start + CHUNK],
            preferred_element_type=F32,
        ).astype(BF16)


def project_stale(blocks, w_qkv, flops):
    rows = len(blocks) * blocks[0].shape[0]
    width, cols = w_qkv.shape
    cols -= width
    return pl.pallas_call(
        stale_kernel,
        in_specs=[pl.BlockSpec(memory_space=pltpu.VMEM)] * (len(blocks) + 1),
        out_specs=pl.BlockSpec(memory_space=pltpu.VMEM),
        out_shape=jax.ShapeDtypeStruct((rows, cols), BF16),
        compiler_params=pltpu.CompilerParams(vmem_limit_bytes=VMEM_LIMIT),
        cost_estimate=pl.CostEstimate(
            flops=flops, bytes_accessed=1, transcendentals=0
        ),
        name="stale_kv",
    )(*blocks, w_qkv)


def gather_kernel(counts, *refs):
    first = 0
    for out_ref, count in zip(refs[sum(counts) :], counts):
        for n in range(count):
            block = refs[first + n]
            rows = block.shape[0]
            out_ref[n * rows : (n + 1) * rows, :] = block[...]
        first += count


def gather_blocks(*groups):
    blocks = [block for group in groups for block in group]
    rows, width = blocks[0].shape
    counts = tuple(len(group) for group in groups)
    vmem = pl.BlockSpec(memory_space=pltpu.VMEM)
    return pl.pallas_call(
        functools.partial(gather_kernel, counts),
        in_specs=[vmem] * len(blocks),
        out_specs=[vmem] * len(groups),
        out_shape=[jax.ShapeDtypeStruct((n * rows, width), BF16) for n in counts],
        compiler_params=pltpu.CompilerParams(vmem_limit_bytes=4 * 1024 * 1024),
        cost_estimate=pl.CostEstimate(
            flops=2 * 10**10, bytes_accessed=4 * 10**7, transcendentals=0
        ),
        name="gather_blocks",
    )(*blocks)


WINDOWS = (
    (0, (0, 1, 2)),
    (128, (3, 4)),
    (256, (5, 6)),
    (384, (7,)),
    (512, (8,)),
    (640, (9, 10, 11)),
    (768, (12,)),
    (896, (13, 14, 15)),
)


def split_stats(stats, lane):
    high = stats.astype(BF16)
    rest = stats - high.astype(F32)
    middle = rest.astype(BF16)
    low = (rest - middle.astype(F32)).astype(BF16)
    split = lane // HEADS
    packed = jnp.where(split == 2, low.astype(F32), 0.0)
    packed = jnp.where(split == 1, middle.astype(F32), packed)
    return jnp.where(split == 0, high.astype(F32), packed)


def attend_part(q_ref, keyval, fresh_ref=None):
    rows = q_ref.shape[0]
    scale = HEAD ** (-0.5)
    lane = lax.broadcasted_iota(jnp.int32, (rows, 256), 1)
    stat_lane = lax.broadcasted_iota(jnp.int32, (rows, STATS), 1)
    stats = jnp.zeros((rows, STATS), F32)
    blocks = [None] * (WIDTH // 128)

    def window(first):
        cols = slice(first, first + 256)
        pieces = [ref[:, cols] for ref in keyval]
        if fresh_ref is not None:
            n_own = fresh_ref.shape[0]
            own = fresh_ref[:, WIDTH + first : WIDTH + first + 256]
            pieces[0:1] = [own, keyval[0][n_own:, cols]]
        return jnp.concatenate(pieces, axis=0)

    def inside(start, head):
        first = head * HEAD - start
        return (lane >= first) & (lane < first + HEAD)

    for part in (WINDOWS,):
        scores = []
        for start, heads in part:
            query = q_ref[:, start : start + 256]
            zero = jnp.zeros((), BF16)
            stack = [jnp.where(inside(start, head), query, zero) for head in heads]
            scores.append(
                lax.dot_general(
                    jnp.concatenate(stack, axis=0),
                    window(start),
                    (((1,), (1,)), ((), ())),
                    preferred_element_type=F32,
                )
            )
        tops = [jnp.max(s, axis=-1, keepdims=True) for s in scores]
        expos = [jnp.exp2((s - t) * (scale * LOG2_E)) for s, t in zip(scores, tops)]
        totals = [jnp.sum(e, axis=-1, keepdims=True) for e in expos]
        for (start, heads), top, expo, total in zip(part, tops, expos, totals):
            value = jnp.dot(
                expo.astype(BF16),
                window(WIDTH + start),
                preferred_element_type=F32,
            )
            value = value * (1.0 / total)
            stat = top * scale + jnp.log(total)
            for n, head in enumerate(heads):
                mine = slice(n * rows, (n + 1) * rows)
                picked = jnp.where(inside(start, head), value[mine], 0.0)
                for j in (0, 1):
                    block = start // 128 + j
                    piece = picked[:, 128 * j : 128 * j + 128]
                    blocks[block] = piece if blocks[block] is None else blocks[block] + piece
                stats = jnp.where(stat_lane % HEADS == head, stat[mine], stats)
    return blocks, stats, stat_lane


def write_packed(out_ref, blocks, stats, lane):
    for block, values in enumerate(blocks):
        out_ref[:, 128 * block : 128 * block + 128] = values.astype(BF16)
    out_ref[:, WIDTH:] = split_stats(stats, lane).astype(BF16)


def attend_early_kernel(q_ref, kv0, kv1, out_ref, stats_ref):
    blocks, stats, _ = attend_part(q_ref, (kv0, kv1))
    for block, values in enumerate(blocks):
        out_ref[:, 128 * block : 128 * block + 128] = values
    stats_ref[...] = stats


def attend_late_kernel(q_ref, kv0, kv1, early_ref, stats_ref, pick_ref, out_ref):
    blocks, stats, lane = attend_part(q_ref, (kv0, kv1))
    first = stats_ref[...]
    top = jnp.maximum(first, stats)
    weights = [jnp.exp(first - top), jnp.exp(stats - top)]
    total = weights[0] + weights[1]
    weights = [split_stats(w / total, lane).astype(BF16) for w in weights]
    pick = pick_ref[...]
    weights = [jnp.dot(w, pick, preferred_element_type=F32) for w in weights]
    mixed = []
    for block, values in enumerate(blocks):
        cols = slice(128 * block, 128 * block + 128)
        mixed.append(weights[0][:, cols] * early_ref[:, cols] + weights[1][:, cols] * values)
    write_packed(out_ref, mixed, top + jnp.log(total), lane)


def attend_cost(rows, keys):
    return pl.CostEstimate(
        flops=4 * HEADS * rows * keys * 256,
        bytes_accessed=4 * keys * WIDTH,
        transcendentals=HEADS * rows * keys,
    )


def attend_early(query, keyval):
    rows = query.shape[0]
    vmem = pl.BlockSpec(memory_space=pltpu.VMEM)
    return pl.pallas_call(
        attend_early_kernel,
        in_specs=[vmem] * 3,
        out_specs=[vmem] * 2,
        out_shape=[
            jax.ShapeDtypeStruct((rows, WIDTH), F32),
            jax.ShapeDtypeStruct((rows, STATS), F32),
        ],
        compiler_params=pltpu.CompilerParams(vmem_limit_bytes=VMEM_LIMIT),
        cost_estimate=pl.CostEstimate(flops=1, bytes_accessed=1, transcendentals=0),
        name="attend_early",
    )(query, *keyval)


def attend_late(query, keyval, first, pick):
    rows = query.shape[0]
    return pl.pallas_call(
        attend_late_kernel,
        in_specs=[pl.BlockSpec(memory_space=pltpu.VMEM)] * 6,
        out_specs=pl.BlockSpec(memory_space=pltpu.VMEM),
        out_shape=jax.ShapeDtypeStruct((rows, WIDTH + STATS), BF16),
        compiler_params=pltpu.CompilerParams(vmem_limit_bytes=VMEM_LIMIT),
        cost_estimate=pl.CostEstimate(flops=1, bytes_accessed=1, transcendentals=0),
        name="attend_late",
    )(query, *keyval, *first, pick)


def attend_own_kernel(
    q_ref, kv0, kv1, kv2, kv3, fresh_ref, time_ref, latent_ref, out_ref, base_ref, gain_ref
):
    image = lax.axis_index("guide")
    now = jnp.full(latent_ref.shape, time_ref[image // 2], jnp.int32)
    bar_now = alpha_bar(now)
    bar_prev = alpha_bar(now - STRIDE)
    latent_gain = jnp.sqrt(bar_prev) / jnp.sqrt(bar_now)
    noise_gain = jnp.sqrt(1.0 - bar_prev) - latent_gain * jnp.sqrt(1.0 - bar_now)
    is_cond = jnp.full(latent_ref.shape, image % 2, jnp.int32) == 0
    base_ref[...] = latent_gain * latent_ref[...]
    gain_ref[0] = noise_gain * jnp.where(is_cond, 4.5, -3.5)
    gain_ref[1] = noise_gain * jnp.where(is_cond, -3.5, 4.5)
    write_packed(out_ref, *attend_part(q_ref, (kv0, kv1, kv2, kv3), fresh_ref))


def attend_own(query, keyval, fresh, timestep, latent):
    rows = query.shape[0]
    vmem = pl.BlockSpec(memory_space=pltpu.VMEM)
    return pl.pallas_call(
        attend_own_kernel,
        in_specs=[vmem] * 6 + [pl.BlockSpec(memory_space=pltpu.SMEM), vmem],
        out_specs=[vmem] * 3,
        out_shape=[
            jax.ShapeDtypeStruct((rows, WIDTH + STATS), BF16),
            jax.ShapeDtypeStruct(latent.shape, F32),
            jax.ShapeDtypeStruct((2, *latent.shape), F32),
        ],
        compiler_params=pltpu.CompilerParams(vmem_limit_bytes=VMEM_LIMIT),
        cost_estimate=attend_cost(rows, sum(x.shape[0] for x in keyval)),
        name="attend_own",
    )(query, *keyval, fresh, timestep, latent)


def post_kernel(
    p0, p1, p2, p3, hidden_ref, mod_ref, w_out_ref, w_final_ref, scaled_ref, gain_ref,
    pick_ref, noise_ref, base_ref,
):
    pick = pick_ref[...]
    parts = (p0, p1, p2, p3)
    sums = [jnp.dot(p[:, WIDTH:], pick, preferred_element_type=F32) for p in parts]
    top = functools.reduce(jnp.maximum, sums)
    weights = [jnp.exp(s - top) for s in sums]
    total = functools.reduce(jnp.add, weights)
    mix = functools.reduce(
        jnp.add, [w * p[:, :WIDTH].astype(F32) for w, p in zip(weights, parts)]
    )
    attended = (mix / total).astype(BF16)
    source = hidden_ref[...].astype(F32)
    mixed = source + mod_ref[2] * jnp.dot(
        attended, w_out_ref[...], preferred_element_type=F32
    )
    final_in = (layer_norm(mixed) * (1.0 + mod_ref[4]) + mod_ref[3]).astype(BF16)
    w_wide = jnp.concatenate([w_final_ref[...]] * 8, axis=0)
    wide = lax.dot_general(
        final_in, w_wide, (((1,), (1,)), ((), ())), preferred_element_type=F32
    )
    rows = wide.shape[0]
    token = lax.broadcasted_iota(jnp.int32, wide.shape, 0) % 8
    place = lax.broadcasted_iota(jnp.int32, wide.shape, 1) // 16
    wide = jnp.where(token == place, wide, 0.0)
    noise = jnp.sum(wide.reshape(rows // 8, 8, 128), axis=1)
    noise_ref[...] = noise
    base_ref[...] = scaled_ref[...] + gain_ref[0] * noise


def post(parts, hidden, mod, w_out, w_final_t, scaled, gain, pick):
    rows = parts[0].shape[0]
    return pl.pallas_call(
        post_kernel,
        in_specs=[pl.BlockSpec(memory_space=pltpu.VMEM)] * 11,
        out_specs=[pl.BlockSpec(memory_space=pltpu.VMEM)] * 2,
        out_shape=[jax.ShapeDtypeStruct(scaled.shape, F32)] * 2,
        compiler_params=pltpu.CompilerParams(vmem_limit_bytes=VMEM_LIMIT),
        cost_estimate=pl.CostEstimate(
            flops=2 * rows * WIDTH * WIDTH, bytes_accessed=2 * WIDTH * WIDTH, transcendentals=0
        ),
        name="post",
    )(*parts, hidden, mod, w_out, w_final_t, scaled, gain, pick)


def body(hidden_in, stale_in, modulation, latent, timestep, w_qkv, w_out, w_final):
    hidden, stale = hidden_in[0], stale_in[0]
    mod = jnp.transpose(modulation, (1, 0, 2))
    rows = hidden.shape[0]

    sent, pick = lax.optimization_barrier((stale, head_selector()))
    stale_1 = send(stale, z_xor(1))
    stale_2, stale_3 = [send(sent, z_xor(mask)) for mask in (2, 3)]
    fresh = project_fresh(hidden, mod, w_qkv)
    query = fresh[:, :WIDTH]
    query_up, query_down, query_far = [send(query, y_shift(step)) for step in (1, -1, 2)]

    early = project_stale([stale, stale_1], w_qkv, 2 * 10**10)
    early_other = send(early, other_core)
    queries, blocks = gather_blocks((query_up, query_down, query_far), (stale_2, stale_3))
    blocks, early_other = lax.optimization_barrier((blocks, early_other))
    late = project_stale([blocks], w_qkv, 1)
    late_other = send(late, other_core)
    keyval = (early, late, early_other, late_other)

    first = attend_early(queries, (early, early_other))
    partial = attend_late(queries, (late, late_other), first, pick)
    back = [
        send(partial[n * rows : (n + 1) * rows], y_shift(step))
        for n, step in enumerate((-1, 1, -2))
    ]
    own, scaled, gain = attend_own(query, keyval, fresh, timestep, latent[0])
    noise, base = post([own] + back, hidden, mod, w_out, w_final.T, scaled, gain, pick)
    partner = lax.ppermute(
        noise, "guide", [(i, i ^ 1) for i in range(lax.axis_size("guide"))]
    )
    return (base + gain[1] * partner)[None]


def solution(mesh):
    in_specs = (
        P("guide", "patch", None),
        P("guide", "patch", None),
        P("guide", None, None),
        P("guide", "patch", None),
        P(),
        P(),
        P(),
        P(),
    )
    out_specs = P("guide", "patch", None)
    return jax.shard_map(body, mesh=mesh, in_specs=in_specs, out_specs=out_specs, check_vma=False)
```

```python
import functools
import math

import jax
import jax.numpy as jnp
from jax import lax
from jax.experimental import pallas as pl
from jax.experimental.pallas import tpu as pltpu
from jax.sharding import PartitionSpec as P

HEADS = 16
HEAD = 72
WIDTH = 1152
STRIDE = 50
NY, NZ, NC = 4, 4, 2
STATS = 128
CHUNK = 384
LOG2_E = 1.4426950408889634
BF16, F32 = jnp.bfloat16, jnp.float32
VMEM_LIMIT = 32 * 1024 * 1024


def layer_norm(values):
    mean = jnp.mean(values, axis=-1, keepdims=True)
    centred = values - mean
    var = jnp.mean(centred * centred, axis=-1, keepdims=True)
    return centred / jnp.sqrt(var + 1e-06)


def alpha_bar(step_index):
    angle = (step_index.astype(F32) / 1000.0 + 0.008) / 1.008 * (math.pi / 2.0)
    return jnp.cos(angle) ** 2


def send(value, route):
    pairs = []
    for y in range(NY):
        for z in range(NZ):
            for c in range(NC):
                ty, tz, tc = route(y, z, c)
                pairs.append(((y * NZ + z) * NC + c, ((ty % NY) * NZ + tz) * NC + tc))
    return lax.ppermute(value, "patch", pairs)


def z_xor(mask):
    return lambda y, z, c: (y, z ^ mask, c)


def other_core(y, z, c):
    return y, z, c ^ 1


def y_shift(step):
    return lambda y, z, c: (y + step, z, c)


def selector_kernel(out_ref):
    row = lax.broadcasted_iota(jnp.int32, (STATS, WIDTH), 0)
    col = lax.broadcasted_iota(jnp.int32, (STATS, WIDTH), 1)
    offset = col - (row % HEADS) * HEAD
    pick = (row < 3 * HEADS) & (offset >= 0) & (offset < HEAD)
    out_ref[...] = jnp.where(pick, 1.0, 0.0).astype(BF16)


def head_selector():
    return pl.pallas_call(
        selector_kernel,
        out_specs=pl.BlockSpec(memory_space=pltpu.VMEM),
        out_shape=jax.ShapeDtypeStruct((STATS, WIDTH), BF16),
        compiler_params=pltpu.CompilerParams(vmem_limit_bytes=4 * 1024 * 1024),
        cost_estimate=pl.CostEstimate(
            flops=2 * 10**10, bytes_accessed=4 * 10**7, transcendentals=0
        ),
        name="head_selector",
    )()


def fresh_kernel(hidden_ref, mod_ref, w_ref, out_ref):
    source = hidden_ref[...].astype(F32)
    attn_in = (layer_norm(source) * (1.0 + mod_ref[1]) + mod_ref[0]).astype(BF16)
    for start in range(0, w_ref.shape[1], CHUNK):
        out_ref[:, start : start + CHUNK] = jnp.dot(
            attn_in, w_ref[:, start : start + CHUNK], preferred_element_type=F32
        ).astype(BF16)


def project_fresh(hidden, mod, w_qkv):
    rows, width = hidden.shape
    cols = w_qkv.shape[1]
    return pl.pallas_call(
        fresh_kernel,
        in_specs=[pl.BlockSpec(memory_space=pltpu.VMEM)] * 3,
        out_specs=pl.BlockSpec(memory_space=pltpu.VMEM),
        out_shape=jax.ShapeDtypeStruct((rows, cols), BF16),
        compiler_params=pltpu.CompilerParams(vmem_limit_bytes=VMEM_LIMIT),
        cost_estimate=pl.CostEstimate(
            flops=2 * rows * width * cols, bytes_accessed=2 * width * cols, transcendentals=0
        ),
        name="fresh_qkv",
    )(hidden, mod, w_qkv)


def stale_kernel(*refs):
    *blocks, w_ref, out_ref = refs
    keys = jnp.concatenate([x[...] for x in blocks], axis=0)
    for start in range(0, out_ref.shape[1], CHUNK):
        out_ref[:, start : start + CHUNK] = jnp.dot(
            keys,
            w_ref[:, WIDTH + start : WIDTH + start + CHUNK],
            preferred_element_type=F32,
        ).astype(BF16)


def project_stale(blocks, w_qkv, flops):
    rows = len(blocks) * blocks[0].shape[0]
    width, cols = w_qkv.shape
    cols -= width
    return pl.pallas_call(
        stale_kernel,
        in_specs=[pl.BlockSpec(memory_space=pltpu.VMEM)] * (len(blocks) + 1),
        out_specs=pl.BlockSpec(memory_space=pltpu.VMEM),
        out_shape=jax.ShapeDtypeStruct((rows, cols), BF16),
        compiler_params=pltpu.CompilerParams(vmem_limit_bytes=VMEM_LIMIT),
        cost_estimate=pl.CostEstimate(
            flops=flops, bytes_accessed=1, transcendentals=0
        ),
        name="stale_kv",
    )(*blocks, w_qkv)


def gather_kernel(counts, *refs):
    first = 0
    for out_ref, count in zip(refs[sum(counts) :], counts):
        for n in range(count):
            block = refs[first + n]
            rows = block.shape[0]
            out_ref[n * rows : (n + 1) * rows, :] = block[...]
        first += count


def gather_blocks(*groups):
    blocks = [block for group in groups for block in group]
    rows, width = blocks[0].shape
    counts = tuple(len(group) for group in groups)
    vmem = pl.BlockSpec(memory_space=pltpu.VMEM)
    return pl.pallas_call(
        functools.partial(gather_kernel, counts),
        in_specs=[vmem] * len(blocks),
        out_specs=[vmem] * len(groups),
        out_shape=[jax.ShapeDtypeStruct((n * rows, width), BF16) for n in counts],
        compiler_params=pltpu.CompilerParams(vmem_limit_bytes=4 * 1024 * 1024),
        cost_estimate=pl.CostEstimate(
            flops=2 * 10**10, bytes_accessed=4 * 10**7, transcendentals=0
        ),
        name="gather_blocks",
    )(*blocks)


WINDOWS = (
    (0, (0, 1, 2)),
    (128, (3, 4)),
    (256, (5, 6)),
    (384, (7,)),
    (512, (8,)),
    (640, (9, 10, 11)),
    (768, (12,)),
    (896, (13, 14, 15)),
)


def split_stats(stats, lane):
    high = stats.astype(BF16)
    rest = stats - high.astype(F32)
    middle = rest.astype(BF16)
    low = (rest - middle.astype(F32)).astype(BF16)
    split = lane // HEADS
    packed = jnp.where(split == 2, low.astype(F32), 0.0)
    packed = jnp.where(split == 1, middle.astype(F32), packed)
    return jnp.where(split == 0, high.astype(F32), packed)


def attend_part(q_ref, keyval, fresh_ref=None):
    rows = q_ref.shape[0]
    scale = HEAD ** (-0.5)
    lane = lax.broadcasted_iota(jnp.int32, (rows, 256), 1)
    stat_lane = lax.broadcasted_iota(jnp.int32, (rows, STATS), 1)
    stats = jnp.zeros((rows, STATS), F32)
    blocks = [None] * (WIDTH // 128)

    def window(first):
        cols = slice(first, first + 256)
        pieces = [ref[:, cols] for ref in keyval]
        if fresh_ref is not None:
            n_own = fresh_ref.shape[0]
            own = fresh_ref[:, WIDTH + first : WIDTH + first + 256]
            pieces[0:1] = [own, keyval[0][n_own:, cols]]
        return jnp.concatenate(pieces, axis=0)

    def inside(start, head):
        first = head * HEAD - start
        return (lane >= first) & (lane < first + HEAD)

    for part in (WINDOWS,):
        scores = []
        for start, heads in part:
            query = q_ref[:, start : start + 256]
            zero = jnp.zeros((), BF16)
            stack = [jnp.where(inside(start, head), query, zero) for head in heads]
            scores.append(
                lax.dot_general(
                    jnp.concatenate(stack, axis=0),
                    window(start),
                    (((1,), (1,)), ((), ())),
                    preferred_element_type=F32,
                )
            )
        tops = [jnp.max(s, axis=-1, keepdims=True) for s in scores]
        expos = [jnp.exp2((s - t) * (scale * LOG2_E)) for s, t in zip(scores, tops)]
        totals = [jnp.sum(e, axis=-1, keepdims=True) for e in expos]
        for (start, heads), top, expo, total in zip(part, tops, expos, totals):
            value = jnp.dot(
                expo.astype(BF16),
                window(WIDTH + start),
                preferred_element_type=F32,
            )
            value = value * (1.0 / total)
            stat = top * scale + jnp.log(total)
            for n, head in enumerate(heads):
                mine = slice(n * rows, (n + 1) * rows)
                picked = jnp.where(inside(start, head), value[mine], 0.0)
                for j in (0, 1):
                    block = start // 128 + j
                    piece = picked[:, 128 * j : 128 * j + 128]
                    blocks[block] = piece if blocks[block] is None else blocks[block] + piece
                stats = jnp.where(stat_lane % HEADS == head, stat[mine], stats)
    return blocks, stats, stat_lane


def write_packed(out_ref, blocks, stats, lane):
    for block, values in enumerate(blocks):
        out_ref[:, 128 * block : 128 * block + 128] = values.astype(BF16)
    out_ref[:, WIDTH:] = split_stats(stats, lane).astype(BF16)


def attend_early_kernel(q_ref, kv0, kv1, out_ref, stats_ref):
    blocks, stats, _ = attend_part(q_ref, (kv0, kv1))
    for block, values in enumerate(blocks):
        out_ref[:, 128 * block : 128 * block + 128] = values
    stats_ref[...] = stats


def attend_late_kernel(q_ref, kv0, kv1, early_ref, stats_ref, pick_ref, out_ref):
    blocks, stats, lane = attend_part(q_ref, (kv0, kv1))
    first = stats_ref[...]
    top = jnp.maximum(first, stats)
    weights = [jnp.exp(first - top), jnp.exp(stats - top)]
    total = weights[0] + weights[1]
    weights = [split_stats(w / total, lane).astype(BF16) for w in weights]
    pick = pick_ref[...]
    rows = lane.shape[0]
    weights = jnp.dot(jnp.concatenate(weights, axis=0), pick, preferred_element_type=F32)
    weights = weights[:rows], weights[rows:]
    mixed = []
    for block, values in enumerate(blocks):
        cols = slice(128 * block, 128 * block + 128)
        mixed.append(weights[0][:, cols] * early_ref[:, cols] + weights[1][:, cols] * values)
    write_packed(out_ref, mixed, top + jnp.log(total), lane)


def attend_cost(rows, keys):
    return pl.CostEstimate(
        flops=4 * HEADS * rows * keys * 256,
        bytes_accessed=4 * keys * WIDTH,
        transcendentals=HEADS * rows * keys,
    )


def attend_early(query, keyval):
    rows = query.shape[0]
    vmem = pl.BlockSpec(memory_space=pltpu.VMEM)
    return pl.pallas_call(
        attend_early_kernel,
        in_specs=[vmem] * 3,
        out_specs=[vmem] * 2,
        out_shape=[
            jax.ShapeDtypeStruct((rows, WIDTH), F32),
            jax.ShapeDtypeStruct((rows, STATS), F32),
        ],
        compiler_params=pltpu.CompilerParams(vmem_limit_bytes=VMEM_LIMIT),
        cost_estimate=pl.CostEstimate(flops=1, bytes_accessed=1, transcendentals=0),
        name="attend_early",
    )(query, *keyval)


def attend_late(query, keyval, first, pick):
    rows = query.shape[0]
    return pl.pallas_call(
        attend_late_kernel,
        in_specs=[pl.BlockSpec(memory_space=pltpu.VMEM)] * 6,
        out_specs=pl.BlockSpec(memory_space=pltpu.VMEM),
        out_shape=jax.ShapeDtypeStruct((rows, WIDTH + STATS), BF16),
        compiler_params=pltpu.CompilerParams(vmem_limit_bytes=VMEM_LIMIT),
        cost_estimate=pl.CostEstimate(flops=1, bytes_accessed=1, transcendentals=0),
        name="attend_late",
    )(query, *keyval, *first, pick)


def attend_own_kernel(
    q_ref, kv0, kv1, kv2, kv3, fresh_ref, time_ref, latent_ref, out_ref, base_ref, gain_ref
):
    image = lax.axis_index("guide")
    now = jnp.full(latent_ref.shape, time_ref[image // 2], jnp.int32)
    bar_now = alpha_bar(now)
    bar_prev = alpha_bar(now - STRIDE)
    latent_gain = jnp.sqrt(bar_prev) / jnp.sqrt(bar_now)
    noise_gain = jnp.sqrt(1.0 - bar_prev) - latent_gain * jnp.sqrt(1.0 - bar_now)
    is_cond = jnp.full(latent_ref.shape, image % 2, jnp.int32) == 0
    base_ref[...] = latent_gain * latent_ref[...]
    gain_ref[0] = noise_gain * jnp.where(is_cond, 4.5, -3.5)
    gain_ref[1] = noise_gain * jnp.where(is_cond, -3.5, 4.5)
    write_packed(out_ref, *attend_part(q_ref, (kv0, kv1, kv2, kv3), fresh_ref))


def attend_own(query, keyval, fresh, timestep, latent):
    rows = query.shape[0]
    vmem = pl.BlockSpec(memory_space=pltpu.VMEM)
    return pl.pallas_call(
        attend_own_kernel,
        in_specs=[vmem] * 6 + [pl.BlockSpec(memory_space=pltpu.SMEM), vmem],
        out_specs=[vmem] * 3,
        out_shape=[
            jax.ShapeDtypeStruct((rows, WIDTH + STATS), BF16),
            jax.ShapeDtypeStruct(latent.shape, F32),
            jax.ShapeDtypeStruct((2, *latent.shape), F32),
        ],
        compiler_params=pltpu.CompilerParams(vmem_limit_bytes=VMEM_LIMIT),
        cost_estimate=attend_cost(rows, sum(x.shape[0] for x in keyval)),
        name="attend_own",
    )(query, *keyval, fresh, timestep, latent)


def post_kernel(
    p0, p1, p2, p3, hidden_ref, mod_ref, w_out_ref, w_final_ref, scaled_ref, gain_ref,
    pick_ref, noise_ref, base_ref,
):
    pick = pick_ref[...]
    parts = (p0, p1, p2, p3)
    rows = p0.shape[0]
    sums = jnp.concatenate([p[:, WIDTH:] for p in parts], axis=0)
    sums = jnp.dot(sums, pick, preferred_element_type=F32)
    sums = [sums[n * rows : (n + 1) * rows] for n in range(len(parts))]
    top = functools.reduce(jnp.maximum, sums)
    weights = [jnp.exp(s - top) for s in sums]
    total = functools.reduce(jnp.add, weights)
    mix = functools.reduce(
        jnp.add, [w * p[:, :WIDTH].astype(F32) for w, p in zip(weights, parts)]
    )
    attended = (mix / total).astype(BF16)
    source = hidden_ref[...].astype(F32)
    mixed = source + mod_ref[2] * jnp.dot(
        attended, w_out_ref[...], preferred_element_type=F32
    )
    final_in = (layer_norm(mixed) * (1.0 + mod_ref[4]) + mod_ref[3]).astype(BF16)
    w_wide = jnp.concatenate([w_final_ref[...]] * 8, axis=0)
    wide = lax.dot_general(
        final_in, w_wide, (((1,), (1,)), ((), ())), preferred_element_type=F32
    )
    token = lax.broadcasted_iota(jnp.int32, wide.shape, 0) % 8
    place = lax.broadcasted_iota(jnp.int32, wide.shape, 1) // 16
    wide = jnp.where(token == place, wide, 0.0)
    noise = jnp.sum(wide.reshape(rows // 8, 8, 128), axis=1)
    noise_ref[...] = noise
    base_ref[...] = scaled_ref[...] + gain_ref[0] * noise


def post(parts, hidden, mod, w_out, w_final_t, scaled, gain, pick):
    rows = parts[0].shape[0]
    return pl.pallas_call(
        post_kernel,
        in_specs=[pl.BlockSpec(memory_space=pltpu.VMEM)] * 11,
        out_specs=[pl.BlockSpec(memory_space=pltpu.VMEM)] * 2,
        out_shape=[jax.ShapeDtypeStruct(scaled.shape, F32)] * 2,
        compiler_params=pltpu.CompilerParams(vmem_limit_bytes=VMEM_LIMIT),
        cost_estimate=pl.CostEstimate(
            flops=2 * rows * WIDTH * WIDTH, bytes_accessed=2 * WIDTH * WIDTH, transcendentals=0
        ),
        name="post",
    )(*parts, hidden, mod, w_out, w_final_t, scaled, gain, pick)


def body(hidden_in, stale_in, modulation, latent, timestep, w_qkv, w_out, w_final):
    hidden, stale = hidden_in[0], stale_in[0]
    mod = jnp.transpose(modulation, (1, 0, 2))
    rows = hidden.shape[0]

    sent, pick = lax.optimization_barrier((stale, head_selector()))
    stale_1 = send(stale, z_xor(1))
    stale_2, stale_3 = [send(sent, z_xor(mask)) for mask in (2, 3)]
    fresh = project_fresh(hidden, mod, w_qkv)
    query = fresh[:, :WIDTH]
    query_up, query_down, query_far = [send(query, y_shift(step)) for step in (1, -1, 2)]

    early = project_stale([stale, stale_1], w_qkv, 2 * 10**10)
    early_other = send(early, other_core)
    queries, blocks = gather_blocks((query_up, query_down, query_far), (stale_2, stale_3))
    blocks, early_other = lax.optimization_barrier((blocks, early_other))
    late = project_stale([blocks], w_qkv, 1)
    late_other = send(late, other_core)
    keyval = (early, late, early_other, late_other)

    first = attend_early(queries, (early, early_other))
    partial = attend_late(queries, (late, late_other), first, pick)
    back = [
        send(partial[n * rows : (n + 1) * rows], y_shift(step))
        for n, step in enumerate((-1, 1, -2))
    ]
    own, scaled, gain = attend_own(query, keyval, fresh, timestep, latent[0])
    noise, base = post([own] + back, hidden, mod, w_out, w_final.T, scaled, gain, pick)
    partner = lax.ppermute(
        noise, "guide", [(i, i ^ 1) for i in range(lax.axis_size("guide"))]
    )
    return (base + gain[1] * partner)[None]


def solution(mesh):
    in_specs = (
        P("guide", "patch", None),
        P("guide", "patch", None),
        P("guide", None, None),
        P("guide", "patch", None),
        P(),
        P(),
        P(),
        P(),
    )
    out_specs = P("guide", "patch", None)
    return jax.shard_map(body, mesh=mesh, in_specs=in_specs, out_specs=out_specs, check_vma=False)
```

```python
import functools
import math

import jax
import jax.numpy as jnp
from jax import lax
from jax.experimental import pallas as pl
from jax.experimental.pallas import tpu as pltpu
from jax.sharding import PartitionSpec as P

HEADS = 16
HEAD = 72
WIDTH = 1152
STRIDE = 50
NY, NZ, NC = 4, 4, 2
STATS = 128
CHUNK = 384
LOG2_E = 1.4426950408889634
BF16, F32 = jnp.bfloat16, jnp.float32
VMEM_LIMIT = 32 * 1024 * 1024


def layer_norm(values):
    mean = jnp.mean(values, axis=-1, keepdims=True)
    centred = values - mean
    var = jnp.mean(centred * centred, axis=-1, keepdims=True)
    return centred * (1.0 / jnp.sqrt(var + 1e-06))


def alpha_bar(step_index):
    angle = (step_index.astype(F32) / 1000.0 + 0.008) / 1.008 * (math.pi / 2.0)
    return jnp.cos(angle) ** 2


def send(value, route):
    pairs = []
    for y in range(NY):
        for z in range(NZ):
            for c in range(NC):
                ty, tz, tc = route(y, z, c)
                pairs.append(((y * NZ + z) * NC + c, ((ty % NY) * NZ + tz) * NC + tc))
    return lax.ppermute(value, "patch", pairs)


def z_xor(mask):
    return lambda y, z, c: (y, z ^ mask, c)


def other_core(y, z, c):
    return y, z, c ^ 1


def y_shift(step):
    return lambda y, z, c: (y + step, z, c)


def selector_kernel(out_ref):
    row = lax.broadcasted_iota(jnp.int32, (STATS, WIDTH), 0)
    col = lax.broadcasted_iota(jnp.int32, (STATS, WIDTH), 1)
    offset = col - (row % HEADS) * HEAD
    pick = (row < 3 * HEADS) & (offset >= 0) & (offset < HEAD)
    out_ref[...] = jnp.where(pick, 1.0, 0.0).astype(BF16)


def head_selector():
    return pl.pallas_call(
        selector_kernel,
        out_specs=pl.BlockSpec(memory_space=pltpu.VMEM),
        out_shape=jax.ShapeDtypeStruct((STATS, WIDTH), BF16),
        compiler_params=pltpu.CompilerParams(vmem_limit_bytes=4 * 1024 * 1024),
        cost_estimate=pl.CostEstimate(
            flops=2 * 10**10, bytes_accessed=4 * 10**7, transcendentals=0
        ),
        name="head_selector",
    )()


def fresh_kernel(hidden_ref, mod_ref, w_ref, out_ref):
    source = hidden_ref[...].astype(F32)
    attn_in = (layer_norm(source) * (1.0 + mod_ref[1]) + mod_ref[0]).astype(BF16)
    for start in range(0, w_ref.shape[1], CHUNK):
        out_ref[:, start : start + CHUNK] = jnp.dot(
            attn_in, w_ref[:, start : start + CHUNK], preferred_element_type=F32
        ).astype(BF16)


def project_fresh(hidden, mod, w_qkv):
    rows, width = hidden.shape
    cols = w_qkv.shape[1]
    return pl.pallas_call(
        fresh_kernel,
        in_specs=[pl.BlockSpec(memory_space=pltpu.VMEM)] * 3,
        out_specs=pl.BlockSpec(memory_space=pltpu.VMEM),
        out_shape=jax.ShapeDtypeStruct((rows, cols), BF16),
        compiler_params=pltpu.CompilerParams(vmem_limit_bytes=VMEM_LIMIT),
        cost_estimate=pl.CostEstimate(
            flops=2 * rows * width * cols, bytes_accessed=2 * width * cols, transcendentals=0
        ),
        name="fresh_qkv",
    )(hidden, mod, w_qkv)


def stale_kernel(*refs):
    *blocks, w_ref, out_ref = refs
    keys = jnp.concatenate([x[...] for x in blocks], axis=0)
    for start in range(0, out_ref.shape[1], CHUNK):
        out_ref[:, start : start + CHUNK] = jnp.dot(
            keys,
            w_ref[:, WIDTH + start : WIDTH + start + CHUNK],
            preferred_element_type=F32,
        ).astype(BF16)


def project_stale(blocks, w_qkv, flops):
    rows = len(blocks) * blocks[0].shape[0]
    width, cols = w_qkv.shape
    cols -= width
    return pl.pallas_call(
        stale_kernel,
        in_specs=[pl.BlockSpec(memory_space=pltpu.VMEM)] * (len(blocks) + 1),
        out_specs=pl.BlockSpec(memory_space=pltpu.VMEM),
        out_shape=jax.ShapeDtypeStruct((rows, cols), BF16),
        compiler_params=pltpu.CompilerParams(vmem_limit_bytes=VMEM_LIMIT),
        cost_estimate=pl.CostEstimate(
            flops=flops, bytes_accessed=1, transcendentals=0
        ),
        name="stale_kv",
    )(*blocks, w_qkv)


def gather_kernel(counts, *refs):
    first = 0
    for out_ref, count in zip(refs[sum(counts) :], counts):
        for n in range(count):
            block = refs[first + n]
            rows = block.shape[0]
            out_ref[n * rows : (n + 1) * rows, :] = block[...]
        first += count


def gather_blocks(*groups):
    blocks = [block for group in groups for block in group]
    rows, width = blocks[0].shape
    counts = tuple(len(group) for group in groups)
    vmem = pl.BlockSpec(memory_space=pltpu.VMEM)
    return pl.pallas_call(
        functools.partial(gather_kernel, counts),
        in_specs=[vmem] * len(blocks),
        out_specs=[vmem] * len(groups),
        out_shape=[jax.ShapeDtypeStruct((n * rows, width), BF16) for n in counts],
        compiler_params=pltpu.CompilerParams(vmem_limit_bytes=4 * 1024 * 1024),
        cost_estimate=pl.CostEstimate(
            flops=2 * 10**10, bytes_accessed=4 * 10**7, transcendentals=0
        ),
        name="gather_blocks",
    )(*blocks)


WINDOWS = (
    (0, (0, 1, 2)),
    (128, (3, 4)),
    (256, (5, 6)),
    (384, (7,)),
    (512, (8,)),
    (640, (9, 10, 11)),
    (768, (12,)),
    (896, (13, 14, 15)),
)


def split_stats(stats, lane):
    high = stats.astype(BF16)
    rest = stats - high.astype(F32)
    middle = rest.astype(BF16)
    low = (rest - middle.astype(F32)).astype(BF16)
    split = lane // HEADS
    packed = jnp.where(split == 2, low.astype(F32), 0.0)
    packed = jnp.where(split == 1, middle.astype(F32), packed)
    return jnp.where(split == 0, high.astype(F32), packed)


def attend_part(q_ref, keyval, fresh_ref=None):
    rows = q_ref.shape[0]
    scale = HEAD ** (-0.5)
    lane = lax.broadcasted_iota(jnp.int32, (rows, 256), 1)
    stat_lane = lax.broadcasted_iota(jnp.int32, (rows, STATS), 1)
    stats = jnp.zeros((rows, STATS), F32)
    blocks = [None] * (WIDTH // 128)

    def window(first):
        cols = slice(first, first + 256)
        pieces = [ref[:, cols] for ref in keyval]
        if fresh_ref is not None:
            n_own = fresh_ref.shape[0]
            own = fresh_ref[:, WIDTH + first : WIDTH + first + 256]
            pieces[0:1] = [own, keyval[0][n_own:, cols]]
        return jnp.concatenate(pieces, axis=0)

    def inside(start, head):
        first = head * HEAD - start
        return (lane >= first) & (lane < first + HEAD)

    for part in (WINDOWS,):
        scores = []
        for start, heads in part:
            query = q_ref[:, start : start + 256]
            zero = jnp.zeros((), BF16)
            stack = [jnp.where(inside(start, head), query, zero) for head in heads]
            scores.append(
                lax.dot_general(
                    jnp.concatenate(stack, axis=0),
                    window(start),
                    (((1,), (1,)), ((), ())),
                    preferred_element_type=F32,
                )
            )
        tops = [jnp.max(s, axis=-1, keepdims=True) for s in scores]
        expos = [jnp.exp2((s - t) * (scale * LOG2_E)) for s, t in zip(scores, tops)]
        totals = [jnp.sum(e, axis=-1, keepdims=True) for e in expos]
        for (start, heads), top, expo, total in zip(part, tops, expos, totals):
            value = jnp.dot(
                expo.astype(BF16),
                window(WIDTH + start),
                preferred_element_type=F32,
            )
            value = value * (1.0 / total)
            stat = top * scale + jnp.log(total)
            for n, head in enumerate(heads):
                mine = slice(n * rows, (n + 1) * rows)
                picked = jnp.where(inside(start, head), value[mine], 0.0)
                for j in (0, 1):
                    block = start // 128 + j
                    piece = picked[:, 128 * j : 128 * j + 128]
                    blocks[block] = piece if blocks[block] is None else blocks[block] + piece
                stats = jnp.where(stat_lane % HEADS == head, stat[mine], stats)
    return blocks, stats, stat_lane


def write_packed(out_ref, blocks, stats, lane):
    for block, values in enumerate(blocks):
        out_ref[:, 128 * block : 128 * block + 128] = values.astype(BF16)
    out_ref[:, WIDTH:] = split_stats(stats, lane).astype(BF16)


def attend_early_kernel(q_ref, kv0, kv1, out_ref, stats_ref):
    blocks, stats, _ = attend_part(q_ref, (kv0, kv1))
    for block, values in enumerate(blocks):
        out_ref[:, 128 * block : 128 * block + 128] = values
    stats_ref[...] = stats


def attend_late_kernel(q_ref, kv0, kv1, early_ref, stats_ref, pick_ref, out_ref):
    blocks, stats, lane = attend_part(q_ref, (kv0, kv1))
    first = stats_ref[...]
    top = jnp.maximum(first, stats)
    weights = [jnp.exp(first - top), jnp.exp(stats - top)]
    total = weights[0] + weights[1]
    weights = [split_stats(w / total, lane).astype(BF16) for w in weights]
    pick = pick_ref[...]
    rows = lane.shape[0]
    weights = jnp.dot(jnp.concatenate(weights, axis=0), pick, preferred_element_type=F32)
    weights = weights[:rows], weights[rows:]
    mixed = []
    for block, values in enumerate(blocks):
        cols = slice(128 * block, 128 * block + 128)
        mixed.append(weights[0][:, cols] * early_ref[:, cols] + weights[1][:, cols] * values)
    write_packed(out_ref, mixed, top + jnp.log(total), lane)


def attend_cost(rows, keys):
    return pl.CostEstimate(
        flops=4 * HEADS * rows * keys * 256,
        bytes_accessed=4 * keys * WIDTH,
        transcendentals=HEADS * rows * keys,
    )


def attend_early(query, keyval):
    rows = query.shape[0]
    vmem = pl.BlockSpec(memory_space=pltpu.VMEM)
    return pl.pallas_call(
        attend_early_kernel,
        in_specs=[vmem] * 3,
        out_specs=[vmem] * 2,
        out_shape=[
            jax.ShapeDtypeStruct((rows, WIDTH), F32),
            jax.ShapeDtypeStruct((rows, STATS), F32),
        ],
        compiler_params=pltpu.CompilerParams(vmem_limit_bytes=VMEM_LIMIT),
        cost_estimate=pl.CostEstimate(flops=1, bytes_accessed=1, transcendentals=0),
        name="attend_early",
    )(query, *keyval)


def attend_late(query, keyval, first, pick):
    rows = query.shape[0]
    return pl.pallas_call(
        attend_late_kernel,
        in_specs=[pl.BlockSpec(memory_space=pltpu.VMEM)] * 6,
        out_specs=pl.BlockSpec(memory_space=pltpu.VMEM),
        out_shape=jax.ShapeDtypeStruct((rows, WIDTH + STATS), BF16),
        compiler_params=pltpu.CompilerParams(vmem_limit_bytes=VMEM_LIMIT),
        cost_estimate=pl.CostEstimate(flops=1, bytes_accessed=1, transcendentals=0),
        name="attend_late",
    )(query, *keyval, *first, pick)


def attend_own_kernel(
    q_ref, kv0, kv1, kv2, kv3, fresh_ref, time_ref, latent_ref, out_ref, base_ref, gain_ref
):
    image = lax.axis_index("guide")
    now = jnp.full(latent_ref.shape, time_ref[image // 2], jnp.int32)
    bar_now = alpha_bar(now)
    bar_prev = alpha_bar(now - STRIDE)
    latent_gain = jnp.sqrt(bar_prev) / jnp.sqrt(bar_now)
    noise_gain = jnp.sqrt(1.0 - bar_prev) - latent_gain * jnp.sqrt(1.0 - bar_now)
    is_cond = jnp.full(latent_ref.shape, image % 2, jnp.int32) == 0
    base_ref[...] = latent_gain * latent_ref[...]
    gain_ref[0] = noise_gain * jnp.where(is_cond, 4.5, -3.5)
    gain_ref[1] = noise_gain * jnp.where(is_cond, -3.5, 4.5)
    write_packed(out_ref, *attend_part(q_ref, (kv0, kv1, kv2, kv3), fresh_ref))


def attend_own(query, keyval, fresh, timestep, latent):
    rows = query.shape[0]
    vmem = pl.BlockSpec(memory_space=pltpu.VMEM)
    return pl.pallas_call(
        attend_own_kernel,
        in_specs=[vmem] * 6 + [pl.BlockSpec(memory_space=pltpu.SMEM), vmem],
        out_specs=[vmem] * 3,
        out_shape=[
            jax.ShapeDtypeStruct((rows, WIDTH + STATS), BF16),
            jax.ShapeDtypeStruct(latent.shape, F32),
            jax.ShapeDtypeStruct((2, *latent.shape), F32),
        ],
        compiler_params=pltpu.CompilerParams(vmem_limit_bytes=VMEM_LIMIT),
        cost_estimate=attend_cost(rows, sum(x.shape[0] for x in keyval)),
        name="attend_own",
    )(query, *keyval, fresh, timestep, latent)


def post_kernel(
    p0, p1, p2, p3, hidden_ref, mod_ref, w_out_ref, w_final_ref, scaled_ref, gain_ref,
    pick_ref, noise_ref, base_ref,
):
    pick = pick_ref[...]
    parts = (p0, p1, p2, p3)
    rows = p0.shape[0]
    sums = jnp.concatenate([p[:, WIDTH:] for p in parts], axis=0)
    sums = jnp.dot(sums, pick, preferred_element_type=F32)
    sums = [sums[n * rows : (n + 1) * rows] for n in range(len(parts))]
    top = functools.reduce(jnp.maximum, sums)
    weights = [jnp.exp(s - top) for s in sums]
    total = functools.reduce(jnp.add, weights)
    mix = functools.reduce(
        jnp.add, [w * p[:, :WIDTH].astype(F32) for w, p in zip(weights, parts)]
    )
    attended = (mix / total).astype(BF16)
    source = hidden_ref[...].astype(F32)
    mixed = source + mod_ref[2] * jnp.dot(
        attended, w_out_ref[...], preferred_element_type=F32
    )
    final_in = (layer_norm(mixed) * (1.0 + mod_ref[4]) + mod_ref[3]).astype(BF16)
    w_wide = jnp.concatenate([w_final_ref[...]] * 8, axis=0)
    wide = lax.dot_general(
        final_in, w_wide, (((1,), (1,)), ((), ())), preferred_element_type=F32
    )
    token = lax.broadcasted_iota(jnp.int32, wide.shape, 0) % 8
    place = lax.broadcasted_iota(jnp.int32, wide.shape, 1) // 16
    wide = jnp.where(token == place, wide, 0.0)
    noise = jnp.sum(wide.reshape(rows // 8, 8, 128), axis=1)
    noise_ref[...] = noise
    base_ref[...] = scaled_ref[...] + gain_ref[0] * noise


def post(parts, hidden, mod, w_out, w_final_t, scaled, gain, pick):
    rows = parts[0].shape[0]
    return pl.pallas_call(
        post_kernel,
        in_specs=[pl.BlockSpec(memory_space=pltpu.VMEM)] * 11,
        out_specs=[pl.BlockSpec(memory_space=pltpu.VMEM)] * 2,
        out_shape=[jax.ShapeDtypeStruct(scaled.shape, F32)] * 2,
        compiler_params=pltpu.CompilerParams(vmem_limit_bytes=VMEM_LIMIT),
        cost_estimate=pl.CostEstimate(
            flops=2 * rows * WIDTH * WIDTH, bytes_accessed=2 * WIDTH * WIDTH, transcendentals=0
        ),
        name="post",
    )(*parts, hidden, mod, w_out, w_final_t, scaled, gain, pick)


def body(hidden_in, stale_in, modulation, latent, timestep, w_qkv, w_out, w_final):
    hidden, stale = hidden_in[0], stale_in[0]
    mod = jnp.transpose(modulation, (1, 0, 2))
    rows = hidden.shape[0]

    sent, pick = lax.optimization_barrier((stale, head_selector()))
    stale_1 = send(stale, z_xor(1))
    stale_2, stale_3 = [send(sent, z_xor(mask)) for mask in (2, 3)]
    fresh = project_fresh(hidden, mod, w_qkv)
    query = fresh[:, :WIDTH]
    query_up, query_down, query_far = [send(query, y_shift(step)) for step in (1, -1, 2)]

    early = project_stale([stale, stale_1], w_qkv, 2 * 10**10)
    early_other = send(early, other_core)
    queries, blocks = gather_blocks((query_up, query_down, query_far), (stale_2, stale_3))
    blocks, early_other = lax.optimization_barrier((blocks, early_other))
    late = project_stale([blocks], w_qkv, 1)
    late_other = send(late, other_core)
    keyval = (early, late, early_other, late_other)

    first = attend_early(queries, (early, early_other))
    partial = attend_late(queries, (late, late_other), first, pick)
    back = [
        send(partial[n * rows : (n + 1) * rows], y_shift(step))
        for n, step in enumerate((-1, 1, -2))
    ]
    own, scaled, gain = attend_own(query, keyval, fresh, timestep, latent[0])
    noise, base = post([own] + back, hidden, mod, w_out, w_final.T, scaled, gain, pick)
    partner = lax.ppermute(
        noise, "guide", [(i, i ^ 1) for i in range(lax.axis_size("guide"))]
    )
    return (base + gain[1] * partner)[None]


def solution(mesh):
    in_specs = (
        P("guide", "patch", None),
        P("guide", "patch", None),
        P("guide", None, None),
        P("guide", "patch", None),
        P(),
        P(),
        P(),
        P(),
    )
    out_specs = P("guide", "patch", None)
    return jax.shard_map(body, mesh=mesh, in_specs=in_specs, out_specs=out_specs, check_vma=False)
```
